256 devices in a mesh: xy: 64 (over x, y, z_lo, core), gz: 4 (over z_hi).
Axes of the slice: x: 4, y: 4, z: 8 (z_hi: 4, z_lo: 2; z = z_hi * 2 + z_lo), core: 2. Of those that a mesh axis runs over, the one named last changes fastest.
Arguments:
- electric: float32 [4, 2048, 2048], P('gz', 'xy'), may hold values from -6 to 6
- magnetic_first: float32 [4, 2048, 2048], P('gz', 'xy'), may hold values from -6 to 6
- magnetic_second: float32 [4, 2048, 2048], P('gz', 'xy'), may hold values from -6 to 6
- region: int32 [4, 2048, 2048], P('gz', 'xy'), may hold values from 0 to 7
- permittivity_table: float32 [8], replicated, may hold values from 1 to 12
- conductivity_table: float32 [8], replicated, may hold values from 0.02 to 4
Outputs:
- electric_final: float32 [4, 2048, 2048], P('gz', 'xy')
- first_final: float32 [4, 2048, 2048], P('gz', 'xy')
- second_final: float32 [4, 2048, 2048], P('gz', 'xy')
The draws below stay inside these ranges and needn't reach their ends.
All inputs are finite; a program needn't handle non-finite values.
Results may differ from the reference program's by a relative error of at most 0.000024.
Values sent between devices are 32-bit elements; how exact they have to be, the bound alone decides.
No kernel may reach another device: no remote copies, remote signals or barrier semaphores. Data moves between devices by JAX's collectives and lax.ppermute only.
A program may use at most 64 MiB of HBM per device.

```python
import math
import jax
import jax.numpy as jnp
from jax import lax

NX = 2048
NY = 2048
REGIONS = 8
NZ = 4


def plant(drawn, own_key, smallest, top_value):
    place = [jax.random.randint(jax.random.fold_in(own_key, axis), (), 0, length) for axis, length in enumerate(drawn.shape)]
    main_axis = drawn.shape.index(max(drawn.shape))
    beside = place[:main_axis] + [(place[main_axis] + 1) % drawn.shape[main_axis]] + place[main_axis + 1:]
    return drawn.at[tuple(place)].set(smallest).at[tuple(beside)].set(top_value)


def level_of(own_key, extent, split, low, high):
    def one(dim, parts):
        heights = jax.random.uniform(jax.random.fold_in(jax.random.fold_in(own_key, 6), dim), (parts,), jnp.float32, low / len(split), high / len(split))
        return jnp.repeat(jnp.exp(heights), extent[dim] // parts).reshape((-1,) + (1,) * (len(extent) - dim - 1))

    gain = one(*split[0])
    for cut in split[1:]:
        gain = gain * one(*cut)
    return gain


def bell_draw(key, dims, width, bound, shards=(), kind=jnp.bfloat16):
    entries = width * jax.random.normal(key, dims, jnp.float32)
    if shards:
        entries = entries * level_of(key, dims, shards, -0.22, 0.18)
    return jnp.clip(entries, -bound, bound).astype(kind)


def setup_inputs(seed: int = 0) -> dict:
    key_list = jax.random.split(jax.random.key(seed), 7)
    electric = bell_draw(key_list[0], (NZ, NY, NX), 1.0, 6.0, ((0, 4), (1, 64)), jnp.float32)
    magnetic_first = bell_draw(key_list[1], (NZ, NY, NX), 1.0, 6.0, ((0, 4), (1, 64)), jnp.float32)
    magnetic_second = bell_draw(key_list[2], (NZ, NY, NX), 1.0, 6.0, ((0, 4), (1, 64)), jnp.float32)
    region = plant(jax.random.randint(key_list[3], (NZ, NY, NX), 0, REGIONS), jax.random.fold_in(key_list[3], 1), 0, REGIONS - 1).astype(jnp.int32)
    permittivity_table = jnp.clip(jnp.exp(jax.random.uniform(key_list[4], (REGIONS,), jnp.float32, math.log(1.0), math.log(12.0))), 1.0, 12.0)
    conductivity_table = jnp.clip(jnp.exp(jax.random.uniform(key_list[5], (REGIONS,), jnp.float32, math.log(0.02), math.log(4.0))), 0.02, 4.0)
    return dict(electric=electric, magnetic_first=magnetic_first, magnetic_second=magnetic_second, region=region, permittivity_table=permittivity_table, conductivity_table=conductivity_table)


time_step = 4.0
vertical_coupling = 0.5

def neighbour(values, axis, step):
    length = values.shape[axis]
    widths = [(0, 0)] * values.ndim
    if step > 0:
        widths[axis] = (0, step)
        begin = step
    else:
        widths[axis] = (-step, 0)
        begin = 0
    padded = jnp.pad(values, widths)
    return lax.slice_in_dim(padded, begin, begin + length, axis=axis)

def vertical(values):
    return neighbour(values, 0, 1) + neighbour(values, 0, -1) - 2.0 * values

def solve_lines(diagonal, right_side):
    length = diagonal.shape[-1]
    index = jnp.arange(length)
    lower_band = jnp.broadcast_to(jnp.where(index > 0, -time_step, 0.0), diagonal.shape[1:]).astype(diagonal.dtype)
    upper_band = jnp.broadcast_to(jnp.where(index < length - 1, -time_step, 0.0), diagonal.shape[1:]).astype(diagonal.dtype)

    def plane(pair):
        solved = lax.linalg.tridiagonal_solve(lower_band, pair[0], upper_band, pair[1][..., None])
        return solved[..., 0]
    return lax.map(plane, (diagonal, right_side))

def reference(electric, magnetic_first, magnetic_second, region, permittivity_table, conductivity_table):
    rate = time_step
    permittivity = permittivity_table[region]
    conductivity = conductivity_table[region]
    dplus = permittivity / time_step + 0.5 * conductivity
    dminus = permittivity / time_step - 0.5 * conductivity
    rhs_one = dminus * electric + (magnetic_second - neighbour(magnetic_second, 2, -1)) - (magnetic_first - neighbour(magnetic_first, 1, -1)) + vertical_coupling * vertical(electric)
    ramp_x = jnp.where(jnp.arange(NX) > 0, 2.0 * rate, rate)
    half_e = solve_lines(dplus + ramp_x, rhs_one)
    half_hy = magnetic_second + rate * (neighbour(half_e, 2, 1) - half_e)
    half_hx = magnetic_first - rate * (neighbour(electric, 1, 1) - electric)
    rhs_two = dminus * half_e + (half_hy - neighbour(half_hy, 2, -1)) - (half_hx - neighbour(half_hx, 1, -1)) + vertical_coupling * vertical(half_e)
    ramp_y = jnp.where(jnp.arange(NY) > 0, 2.0 * rate, rate)
    swapped_rhs = jnp.transpose(rhs_two, (0, 2, 1))
    swapped_dplus = jnp.transpose(dplus, (0, 2, 1))
    full_e = solve_lines(swapped_dplus + ramp_y, swapped_rhs)
    swapped_hx = jnp.transpose(half_hx, (0, 2, 1))
    full_hx = swapped_hx - rate * (neighbour(full_e, 2, 1) - full_e)
    full_hy = half_hy + rate * (neighbour(half_e, 2, 1) - half_e)
    return (full_e, full_hx, jnp.transpose(full_hy, (0, 2, 1)))
```

```python
import jax
import jax.numpy as jnp
from jax import lax
from jax.experimental import pallas as pl
from jax.experimental.pallas import tpu as pltpu
from jax.sharding import PartitionSpec as P

RATE = 4.0
KAPPA = 0.5
ROWS = 32
LINE = 2048
PEERS = 64
TILES = LINE // 128
F32 = jnp.float32


def lanes():
    return lax.broadcasted_iota(jnp.int32, (8, 128), 1)


def swap_blocks(tiles, lane):
    left = lane < 64
    even = (lane & 32) == 0
    half = [None] * 4
    for low in range(2):
        a, b = tiles[low], tiles[low + 2]
        half[low] = jnp.where(left, a, pltpu.roll(b, 64, 1))
        half[low + 2] = jnp.where(left, pltpu.roll(a, 64, 1), b)
    out = [None] * 4
    for high in (0, 2):
        a, b = half[high], half[high + 1]
        out[high] = jnp.where(even, a, pltpu.roll(b, 32, 1))
        out[high + 1] = jnp.where(even, pltpu.roll(a, 96, 1), b)
    return out


def pack(source, target, first):
    lane = lanes()
    for wide in range(4):
        square = jnp.concatenate(
            [source[:, pl.ds(512 * wide + 128 * q, 128)] for q in range(4)], axis=0
        ).T
        for b in range(4):
            tiles = [square[32 * b + 8 * t : 32 * b + 8 * t + 8, :] for t in range(4)]
            for q, tile in enumerate(swap_blocks(tiles, lane)):
                target[16 * wide + 4 * q + b, pl.ds(first, 8), :] = tile


def unpack(source, first, target):
    lane = lanes()
    for g in range(TILES):
        tiles = [source[4 * g + s, pl.ds(first, 8), :] for s in range(4)]
        for t, tile in enumerate(swap_blocks(tiles, lane)):
            target[pl.ds(8 * t, 8), pl.ds(128 * g, 128)] = tile


def from_before(values, step, lane):
    if step >= 128:
        jump = step // 128
        return [None] * jump + values[: TILES - jump]
    turned = [pltpu.roll(v, step, 1) for v in values]
    edge = lane < step
    return [
        jnp.where(edge, turned[k - 1] if k else 0.0, turned[k]) for k in range(TILES)
    ]


def from_after(values, step, lane):
    if step >= 128:
        jump = step // 128
        return values[jump:] + [None] * jump
    turned = [pltpu.roll(v, 128 - step, 1) for v in values]
    edge = lane >= 128 - step
    return [
        jnp.where(edge, turned[k + 1] if k + 1 < TILES else 0.0, turned[k])
        for k in range(TILES)
    ]


def plus(a, b):
    return a if b is None else a + b


def minus(a, b):
    return a if b is None else a - b


def times(a, b):
    return None if a is None or b is None else a * b


def solve(diagonal, right, lane):
    weight = [1.0 / d for d in diagonal]
    share = [w * r for w, r in zip(weight, right)]
    weight_before = from_before(weight, 1, lane)
    weight_after = from_after(weight, 1, lane)
    share_before = from_before(share, 1, lane)
    share_after = from_after(share, 1, lane)
    square = RATE * RATE
    couple = [square * w for w in weight_before]
    couple[0] = jnp.where(lane >= 2, couple[0], 0.0)
    diagonal = [
        d - square * (a + b) for d, a, b in zip(diagonal, weight_before, weight_after)
    ]
    right = [r + RATE * (a + b) for r, a, b in zip(right, share_before, share_after)]
    step = 2
    while step < LINE:
        weight = [1.0 / d for d in diagonal]
        share = [w * r for w, r in zip(weight, right)]
        pull = [times(w, c) for w, c in zip(weight, couple)]
        back_r = [times(c, h) for c, h in zip(couple, share)]
        back_d = [times(c, g) for c, g in zip(couple, pull)]
        share_before = from_before(share, step, lane)
        weight_before = from_before(weight, step, lane)
        pull_before = from_before(pull, step, lane)
        back_r = from_after(back_r, step, lane)
        back_d = from_after(back_d, step, lane)
        right = [
            plus(plus(r, times(c, h)), b)
            for r, c, h, b in zip(right, couple, share_before, back_r)
        ]
        diagonal = [
            minus(minus(d, times(c, times(c, w))), b)
            for d, c, w, b in zip(diagonal, couple, weight_before, back_d)
        ]
        couple = [times(c, g) for c, g in zip(couple, pull_before)]
        step *= 2
    return [r / d for r, d in zip(right, diagonal)]


def read(ref, group):
    return [ref[pl.ds(group, 8), pl.ds(128 * k, 128)] for k in range(TILES)]


def write(ref, group, values):
    for k, v in enumerate(values):
        ref[pl.ds(group, 8), pl.ds(128 * k, 128)] = v


def ramp(values, lane):
    out = [v + 2.0 * RATE for v in values]
    out[0] = values[0] + jnp.where(lane > 0, 2.0 * RATE, RATE)
    return out


def prepare_kernel(
    e_ref, hx_ref, hy_ref, region_ref, eps_ref, sig_ref, below_ref, above_ref,
    early_ref, dplus_ref, dminus_ref, base_ref, drop_ref, half_hx_ref,
):
    region = region_ref[...]
    dplus = jnp.zeros(region.shape, F32)
    dminus = jnp.zeros(region.shape, F32)
    for entry in range(8):
        eps = eps_ref[entry] / RATE
        sig = 0.5 * sig_ref[entry]
        here = region == entry
        dplus = jnp.where(here, eps + sig, dplus)
        dminus = jnp.where(here, eps - sig, dminus)
    dplus_ref[...] = dplus
    dminus_ref[...] = dminus
    e = e_ref[...]
    hx = hx_ref[...]
    hy = hy_ref[...]
    row = lax.broadcasted_iota(jnp.int32, (ROWS, LINE), 0)
    column = lax.broadcasted_iota(jnp.int32, (ROWS, LINE), 1)
    hx_below = below_ref[0:1, :]
    e_below = below_ref[1:2, :]
    hx_prev = jnp.where(row == 0, hx_below, pltpu.roll(hx, 1, 0))
    e_next = jnp.where(row == ROWS - 1, above_ref[...], pltpu.roll(e, ROWS - 1, 0))
    hy_prev = jnp.where(column == 0, 0.0, pltpu.roll(hy, 1, 1))
    base_ref[...] = dminus * e + (hy - hy_prev) - (hx - hx_prev) - (2.0 * KAPPA) * e
    half_hx = hx - RATE * (e_next - e)
    half_hx_ref[...] = half_hx
    edge = hx_below - RATE * (e[0:1, :] - e_below)
    edge = jnp.where(lax.axis_index("xy") > 0, edge, 0.0)
    half_prev = jnp.where(row == 0, edge, pltpu.roll(half_hx, 1, 0))
    drop_ref[...] = half_hx - half_prev
    pack(dplus_ref, early_ref, 0)
    pack(half_hx_ref, early_ref, 8)


def first_kernel(
    base_ref, up_ref, down_ref, dplus_ref, dminus_ref, drop_ref, hy_ref,
    half_ref, base_two_ref, full_hy_ref, e_scr, b_scr, h_scr,
):
    lane = lanes()

    def body(i, carry):
        group = pl.multiple_of(8 * i, 8)
        right = [
            b + KAPPA * (u + d)
            for b, u, d in zip(read(base_ref, group), read(up_ref, group), read(down_ref, group))
        ]
        half = solve(ramp(read(dplus_ref, group), lane), right, lane)
        write(e_scr, group, half)
        hy = read(hy_ref, group)
        step = [RATE * (a - h) for a, h in zip(from_after(half, 1, lane), half)]
        half_hy = [a + b for a, b in zip(hy, step)]
        write(h_scr, group, [a + b for a, b in zip(half_hy, step)])
        before = from_before(half_hy, 1, lane)
        write(
            b_scr,
            group,
            [
                m * h + (a - b) - d - (2.0 * KAPPA) * h
                for m, h, a, b, d in zip(
                    read(dminus_ref, group), half, half_hy, before, read(drop_ref, group)
                )
            ],
        )
        return carry

    lax.fori_loop(0, 4, body, 0)
    pack(e_scr, half_ref, 0)
    pack(b_scr, base_two_ref, 0)
    pack(h_scr, full_hy_ref, 0)


def merge_kernel(base_ref, up_ref, down_ref, hy_ref, out_ref):
    out_ref[:, pl.ds(0, 8), :] = base_ref[...] + KAPPA * (up_ref[...] + down_ref[...])
    out_ref[:, pl.ds(8, 8), :] = hy_ref[...]


def second_kernel(early_ref, late_ref, e_ref, hx_ref, hy_ref, d_scr, r_scr):
    lane = lanes()
    unpack(early_ref, 0, d_scr)
    unpack(early_ref, 8, hx_ref)
    unpack(late_ref, 0, r_scr)
    unpack(late_ref, 8, hy_ref)

    def body(i, carry):
        group = pl.multiple_of(8 * i, 8)
        full = solve(ramp(read(d_scr, group), lane), read(r_scr, group), lane)
        write(e_ref, group, full)
        after = from_after(full, 1, lane)
        hx = read(hx_ref, group)
        write(hx_ref, group, [h - RATE * (a - f) for h, a, f in zip(hx, after, full)])
        return carry

    lax.fori_loop(0, 4, body, 0)


def passed(value, axis, step):
    count = lax.axis_size(axis)
    pairs = [(i, i + step) for i in range(count) if 0 <= i + step < count]
    return lax.ppermute(value, axis, pairs)


VMEM = pl.BlockSpec(memory_space=pltpu.VMEM)
SMEM = pl.BlockSpec(memory_space=pltpu.SMEM)
PARAMS = pltpu.CompilerParams(vmem_limit_bytes=32 * 1024 * 1024)


def struct(*shape):
    return jax.ShapeDtypeStruct(shape, F32)


def exchanged(value):
    return lax.all_to_all(value, "xy", split_axis=0, concat_axis=0, tiled=True)


def local(electric, magnetic_first, magnetic_second, region, eps, sig):
    plane = (ROWS, LINE)
    packed = (PEERS, 8, 128)
    e = electric.reshape(plane)
    hx = magnetic_first.reshape(plane)
    hy = magnetic_second.reshape(plane)
    up = passed(e, "gz", 1)
    down = passed(e, "gz", -1)
    below = passed(jnp.concatenate([hx[-1:], e[-1:]], axis=0), "xy", 1)
    above = passed(e[:1], "xy", -1)
    early, dplus, dminus, base, drop, _ = pl.pallas_call(
        prepare_kernel,
        out_shape=(struct(PEERS, 16, 128),) + (struct(*plane),) * 5,
        in_specs=[VMEM] * 4 + [SMEM] * 2 + [VMEM] * 2,
        out_specs=(VMEM,) * 6,
        compiler_params=PARAMS,
        name="prepare",
    )(e, hx, hy, region.reshape(plane), eps, sig, below, above)
    early = exchanged(early)
    half, base_two, full_hy = pl.pallas_call(
        first_kernel,
        out_shape=(struct(*packed),) * 3,
        in_specs=[VMEM] * 7,
        out_specs=(VMEM,) * 3,
        scratch_shapes=[pltpu.VMEM(plane, F32)] * 3,
        compiler_params=PARAMS,
        name="first",
    )(base, up, down, dplus, dminus, drop, hy)
    half_up = passed(half, "gz", 1)
    half_down = passed(half, "gz", -1)
    late = pl.pallas_call(
        merge_kernel,
        out_shape=struct(PEERS, 16, 128),
        in_specs=[VMEM] * 4,
        out_specs=VMEM,
        compiler_params=PARAMS,
        name="merge",
    )(base_two, half_up, half_down, full_hy)
    late = exchanged(late)
    out = pl.pallas_call(
        second_kernel,
        out_shape=(struct(*plane),) * 3,
        in_specs=[VMEM] * 2,
        out_specs=(VMEM,) * 3,
        scratch_shapes=[pltpu.VMEM(plane, F32)] * 2,
        compiler_params=PARAMS,
        name="second",
    )(early, late)
    return tuple(o.reshape(1, ROWS, LINE) for o in out)


def solution(mesh):
    field = P("gz", "xy", None)
    return jax.shard_map(
        local,
        mesh=mesh,
        in_specs=(field,) * 4 + (P(), P()),
        out_specs=(field,) * 3,
        check_vma=False,
    )
```

```python
import jax
import jax.numpy as jnp
from jax import lax
from jax.experimental import pallas as pl
from jax.experimental.pallas import tpu as pltpu
from jax.sharding import PartitionSpec as P

RATE = 4.0
KAPPA = 0.5
ROWS = 32
LINE = 2048
PEERS = 64
TILES = LINE // 128
F32 = jnp.float32
LEVELS = 11
SEGMENT = 8
GROUPS = 8
CUT_LEVELS = 8


def index(shape, axis):
    return lax.broadcasted_iota(jnp.int32, shape, axis)


def swap_blocks(tiles, lane):
    left = lane < 64
    even = (lane & 32) == 0
    half = [None] * 4
    for low in range(2):
        a, b = tiles[low], tiles[low + 2]
        half[low] = jnp.where(left, a, pltpu.roll(b, 64, 1))
        half[low + 2] = jnp.where(left, pltpu.roll(a, 64, 1), b)
    out = [None] * 4
    for high in (0, 2):
        a, b = half[high], half[high + 1]
        out[high] = jnp.where(even, a, pltpu.roll(b, 32, 1))
        out[high + 1] = jnp.where(even, pltpu.roll(a, 96, 1), b)
    return out


def pack(source, target, first):
    lane = index((8, 128), 1)
    for q in range(TILES):
        tiles = [source[8 * u : 8 * u + 8, 128 * q : 128 * q + 128] for u in range(4)]
        for b, tile in enumerate(swap_blocks(tiles, lane)):
            target[4 * q + b, first : first + 8, :] = tile


def turned(tile_of, lane):
    for wide in range(4):
        columns = []
        for s in range(4):
            columns += swap_blocks([tile_of(16 * wide + 4 * g + s) for g in range(4)], lane)
        square = jnp.concatenate(columns, axis=0).T
        for g in range(4):
            yield 128 * (4 * wide + g), square[32 * g : 32 * g + 32, :]


def from_before(values, step, lane):
    if step >= 128:
        jump = step // 128
        return [None] * jump + values[: TILES - jump]
    moved = [pltpu.roll(v, step, 1) for v in values]
    edge = lane < step
    return [jnp.where(edge, moved[k - 1] if k else 0.0, moved[k]) for k in range(TILES)]


def from_after(values, step, lane, wrap=False):
    if step >= 128:
        jump = step // 128
        return values[jump:] + [None] * jump
    moved = [pltpu.roll(v, 128 - step, 1) for v in values]
    edge = lane >= 128 - step
    moved.append(moved[0] if wrap else 0.0)
    return [jnp.where(edge, moved[k + 1], moved[k]) for k in range(TILES)]


def cut_before(values, step):
    if step >= 32:
        jump = step // 32
        return [None] * jump + values[: GROUPS - jump]
    row, lane = index((8, 128), 0), index((8, 128), 1)
    if step >= 4:
        count = step // 4
        moved = [pltpu.roll(v, count, 0) for v in values]
        edge = row < count
        return [jnp.where(edge, moved[k - 1] if k else 0.0, moved[k]) for k in range(GROUPS)]
    aside = [pltpu.roll(v, 32 * step, 1) for v in values]
    moved = [pltpu.roll(v, 1, 0) for v in aside]
    edge = row < 1
    return [
        jnp.where(
            lane < 32 * step,
            jnp.where(edge, moved[k - 1] if k else 0.0, moved[k]),
            aside[k],
        )
        for k in range(GROUPS)
    ]


def cut_after(values, step, wrap=False):
    if step >= 32:
        jump = step // 32
        return values[jump:] + [None] * jump
    row, lane = index((8, 128), 0), index((8, 128), 1)
    if step >= 4:
        count = step // 4
        moved = [pltpu.roll(v, 8 - count, 0) for v in values] + [0.0]
        edge = row >= 8 - count
        return [jnp.where(edge, moved[k + 1], moved[k]) for k in range(GROUPS)]
    aside = [pltpu.roll(v, 128 - 32 * step, 1) for v in values]
    moved = [pltpu.roll(v, 7, 0) for v in aside]
    moved.append(moved[0] if wrap else 0.0)
    edge = row >= 7
    return [
        jnp.where(
            lane >= 128 - 32 * step, jnp.where(edge, moved[k + 1], moved[k]), aside[k]
        )
        for k in range(GROUPS)
    ]


def minus(a, b):
    return a if b is None else a - b


def times(a, b):
    return None if a is None or b is None else a * b


def read(ref):
    return [ref[:, 128 * k : 128 * k + 128] for k in range(TILES)]


def write(ref, values):
    for k, v in enumerate(values):
        ref[:, 128 * k : 128 * k + 128] = v


def factor_level(diagonal, couple, step, before, after):
    weight = [1.0 / d for d in diagonal]
    pull = [times(w, c) for w, c in zip(weight, couple)]
    low = [times(c, w) for c, w in zip(couple, before(weight, step))]
    high = after(pull, step)
    loss = after([times(c, g) for c, g in zip(couple, pull)], step)
    diagonal = [
        minus(minus(d, times(c, a)), b) for d, c, a, b in zip(diagonal, couple, low, loss)
    ]
    couple = [times(a, c) for a, c in zip(low, before(couple, step))]
    return diagonal, couple, low, high


def reduce_level(right, low, high, step, before, after):
    out = []
    for r, a, b, x, y in zip(right, low, high, before(right, step), after(right, step)):
        if x is not None:
            r = r + a * x
        if y is not None:
            r = r + b * y
        out.append(r)
    return out


def factor_lines(diagonal, lane, coef_ref):
    def store(at, values):
        for k, v in enumerate(values):
            if v is not None:
                coef_ref[at, :, 128 * k : 128 * k + 128] = v

    def before(values, step):
        return from_before(values, step, lane)

    def after(values, step):
        return from_after(values, step, lane)

    square = RATE * RATE
    weight = [1.0 / d for d in diagonal]
    left, right = before(weight, 1), after(weight, 1)
    store(0, [RATE * w for w in left])
    store(1, [RATE * w for w in right])
    diagonal = [d - square * (a + b) for d, a, b in zip(diagonal, left, right)]
    couple = [square * w for w in left]
    couple[0] = jnp.where(lane >= 2, couple[0], 0.0)
    for level in range(1, LEVELS):
        diagonal, couple, low, high = factor_level(diagonal, couple, 1 << level, before, after)
        store(2 * level, low)
        store(2 * level + 1, high)
    store(2 * LEVELS, [1.0 / d for d in diagonal])


def reduce_lines(right, lane, coef_ref):
    def load(at):
        return [coef_ref[at, :, 128 * k : 128 * k + 128] for k in range(TILES)]

    def before(values, step):
        return from_before(values, step, lane)

    def after(values, step):
        return from_after(values, step, lane)

    for level in range(LEVELS):
        right = reduce_level(right, load(2 * level), load(2 * level + 1), 1 << level, before, after)
    return [r * w for r, w in zip(right, load(2 * LEVELS))]


def rows_kernel(e_ref, hx_ref, below_ref, e_scr, hx_scr, sem):
    tail = pl.ds(ROWS - 8, 8)
    copies = [
        pltpu.make_async_copy(hx_ref.at[tail], hx_scr, sem.at[0]),
        pltpu.make_async_copy(e_ref.at[tail], e_scr, sem.at[1]),
    ]
    for c in copies:
        c.start()
    for c in copies:
        c.wait()
    below_ref[0:1, :] = hx_scr[7:8, :]
    below_ref[1:2, :] = e_scr[7:8, :]


def send_kernel(
    region_hbm, e_hbm, hx_hbm, eps_ref, sig_ref, below_ref,
    early_ref, dplus_ref, dminus_ref, e_ref, hx_ref,
    region_ref, shifted_ref, sem,
):
    copies = [
        pltpu.make_async_copy(region_hbm, region_ref, sem.at[0]),
        pltpu.make_async_copy(e_hbm, e_ref, sem.at[1]),
        pltpu.make_async_copy(hx_hbm, hx_ref, sem.at[2]),
    ]
    for c in copies:
        c.start()
    plus_table = []
    minus_table = []
    for entry in range(8):
        eps = eps_ref[entry] / RATE
        sig = 0.5 * sig_ref[entry]
        plus_table.append(eps + sig)
        minus_table.append(eps - sig)
    row = index((ROWS, 128), 0)
    inside = lax.axis_index("xy") > 0
    for c in copies:
        c.wait()
    for k, here in enumerate(read(region_ref)):
        at = pl.ds(128 * k, 128)
        a = jnp.full((ROWS, 128), plus_table[0])
        b = jnp.full((ROWS, 128), minus_table[0])
        for entry in range(1, 8):
            mask = here == entry
            a = jnp.where(mask, plus_table[entry], a)
            b = jnp.where(mask, minus_table[entry], b)
        dplus_ref[:, at] = a
        dminus_ref[:, at] = b
        e = e_ref[:, at]
        edge = below_ref[0:1, at] - RATE * (jnp.where(inside, e[0:1], 0.0) - below_ref[1:2, at])
        half_hx = hx_ref[:, at] - RATE * (pltpu.roll(e, ROWS - 1, 0) - e)
        shifted_ref[:, at] = jnp.where(row == 0, edge, pltpu.roll(half_hx, 1, 0))
    pack(dplus_ref, early_ref, 0)
    pack(shifted_ref, early_ref, 8)


def start_kernel(
    dplus_ref, dminus_ref, e_ref, hx_ref, hy_hbm, below_ref, coef_ref, base_ref, hy_ref, sem
):
    copy = pltpu.make_async_copy(hy_hbm, hy_ref, sem)
    copy.start()
    lane = index((ROWS, 128), 1)
    row = index((ROWS, 128), 0)
    diagonal = [
        d + (2.0 * RATE if k else jnp.where(lane > 0, 2.0 * RATE, RATE))
        for k, d in enumerate(read(dplus_ref))
    ]
    factor_lines(diagonal, lane, coef_ref)
    inside = lax.axis_index("xy") > 0
    copy.wait()
    hy_before = from_before(read(hy_ref), 1, lane)
    for k in range(TILES):
        at = pl.ds(128 * k, 128)
        hx = hx_ref[:, at]
        edge = jnp.where(inside, below_ref[0:1, at], 0.0)
        hx_before = jnp.where(row == 0, edge, pltpu.roll(hx, 1, 0))
        e = e_ref[:, at]
        base_ref[:, at] = (
            dminus_ref[:, at] * e + (hy_ref[:, at] - hy_before[k]) - (hx - hx_before) - (2.0 * KAPPA) * e
        )


def first_kernel(base_ref, up_ref, down_ref, coef_ref, half_ref, packed_ref):
    lane = index((ROWS, 128), 1)
    right = [
        b + KAPPA * (u + d) for b, u, d in zip(read(base_ref), read(up_ref), read(down_ref))
    ]
    write(half_ref, reduce_lines(right, lane, coef_ref))
    pack(half_ref, packed_ref, 0)


def between_kernel(half_ref, dminus_ref, hy_ref, base_ref, full_hy_ref, b_scr, h_scr):
    lane = index((ROWS, 128), 1)
    half = read(half_ref)
    change = [RATE * (a - h) for a, h in zip(from_after(half, 1, lane), half)]
    half_hy = [a + b for a, b in zip(read(hy_ref), change)]
    write(h_scr, [a + b for a, b in zip(half_hy, change)])
    hy_before = from_before(half_hy, 1, lane)
    for k, (m, h) in enumerate(zip(read(dminus_ref), half)):
        b_scr[:, 128 * k : 128 * k + 128] = m * h + (half_hy[k] - hy_before[k]) - (2.0 * KAPPA) * h
    pack(h_scr, full_hy_ref, 0)
    pack(b_scr, base_ref, 0)


def merge_kernel(hy_ref, base_ref, up_ref, down_ref, late_ref):
    late_ref[:, 0:8, :] = base_ref[...] + KAPPA * (up_ref[...] + down_ref[...])
    late_ref[:, 8:16, :] = hy_ref[...]


def lines_kernel(early_ref, forth_ref, back_ref, cut_ref, drop_ref, hx_ref):
    lane = index((8, 128), 1)
    row = index((8, 128), 0)

    def tiles(which):
        return lambda s: early_ref[16 * s + 8 * which : 16 * s + 8 * which + 8, :]

    def cells(which, v):
        return [early_ref[pl.ds(128 * g + 8 * which + v, 8, stride=16), :] for g in range(GROUPS)]

    blocks = [block for _, block in turned(tiles(1), lane)]
    write(hx_ref, from_after(blocks, 1, index((ROWS, 128), 1), wrap=True))

    def put(ref, at, values):
        for g, value in enumerate(values):
            if value is not None:
                ref[at, 8 * g : 8 * g + 8, :] = value

    first_segment = (row == 0) & (lane < 32)
    shifted = [cells(1, v) for v in range(SEGMENT)]
    after = cut_after(shifted[0], 1, wrap=True)
    shifted.append(after)
    for v in range(SEGMENT):
        before = list(shifted[v])
        if v == 0:
            before[0] = jnp.where(first_segment, 0.0, before[0])
        put(drop_ref, v, [a - b for a, b in zip(shifted[v + 1], before)])

    diagonal = [[d + 2.0 * RATE for d in cells(0, v)] for v in range(SEGMENT)]
    diagonal[0][0] = diagonal[0][0] - jnp.where(first_segment, RATE, 0.0)
    inner = SEGMENT - 1
    forth = [RATE / d for d in diagonal[0]]
    put(forth_ref, 0, forth)
    product = forth
    for v in range(1, inner):
        forth = [RATE / (d - RATE * p) for d, p in zip(diagonal[v], forth)]
        put(forth_ref, v, forth)
        product = [a * b for a, b in zip(product, forth)]
    back = [RATE / d for d in diagonal[inner - 1]]
    put(back_ref, inner - 1, back)
    for v in range(inner - 2, -1, -1):
        back = [RATE / (d - RATE * p) for d, p in zip(diagonal[v], back)]
        put(back_ref, v, back)
    couple = [RATE * p for p in product]
    couple[0] = jnp.where(first_segment, 0.0, couple[0])
    diagonal = [
        d - RATE * (a + b) for d, a, b in zip(diagonal[inner], forth, cut_after(back, 1))
    ]
    for level in range(CUT_LEVELS):
        diagonal, couple, low, high = factor_level(
            diagonal, couple, 1 << level, cut_before, cut_after
        )
        put(cut_ref, 2 * level, low)
        put(cut_ref, 2 * level + 1, high)
    put(cut_ref, 2 * CUT_LEVELS, [1.0 / d for d in diagonal])


def second_kernel(
    late_ref, forth_ref, back_ref, cut_ref, drop_ref, half_hx_ref, e_ref, hx_ref, hy_ref, full_scr
):
    def get(ref, at):
        return [ref[at, 8 * g : 8 * g + 8, :] for g in range(GROUPS)]

    inner = SEGMENT - 1
    right = [
        [
            late_ref[pl.ds(128 * g + v, 8, stride=16), :] - d
            for g, d in enumerate(get(drop_ref, v))
        ]
        for v in range(SEGMENT)
    ]
    forth = [p * r for p, r in zip(get(forth_ref, 0), right[0])]
    back = [p * r for p, r in zip(get(back_ref, inner - 1), right[inner - 1])]
    for v in range(1, inner):
        forth = [p * (r + u) for p, r, u in zip(get(forth_ref, v), right[v], forth)]
        w = inner - 1 - v
        back = [p * (r + u) for p, r, u in zip(get(back_ref, w), right[w], back)]
    between = [r + a + b for r, a, b in zip(right[inner], forth, cut_after(back, 1))]
    for level in range(CUT_LEVELS):
        between = reduce_level(
            between, get(cut_ref, 2 * level), get(cut_ref, 2 * level + 1), 1 << level, cut_before, cut_after
        )
    between = [r * w for r, w in zip(between, get(cut_ref, 2 * CUT_LEVELS))]

    def put(v, values):
        for g, value in enumerate(values):
            full_scr[pl.ds(64 * g + v, 8, stride=8), :] = value

    put(inner, between)
    scaled = [RATE * s for s in between]
    chain = [cut_before(scaled, 1)]
    for v in range(inner):
        chain.append([p * (r + u) for p, r, u in zip(get(forth_ref, v), right[v], chain[-1])])
    after = scaled
    for v in range(inner - 1, -1, -1):
        after = [u + p * x for u, p, x in zip(chain[v + 1], get(forth_ref, v), after)]
        put(v, [x * (1.0 / RATE) for x in after])

    for at, block in turned(lambda s: late_ref[16 * s + 8 : 16 * s + 16, :], index((8, 128), 1)):
        hy_ref[:, at : at + 128] = block
    full = []
    for at, block in turned(lambda s: full_scr[8 * s : 8 * s + 8, :], index((8, 128), 1)):
        e_ref[:, at : at + 128] = block
        full.append(block)
    after = from_after(full, 1, index((ROWS, 128), 1))
    write(hx_ref, [h - RATE * (a - f) for h, a, f in zip(read(half_hx_ref), after, full)])


VMEM = pl.BlockSpec(memory_space=pltpu.VMEM)
SMEM = pl.BlockSpec(memory_space=pltpu.SMEM)
HBM = pl.BlockSpec(memory_space=pltpu.HBM)


def struct(*shape):
    return jax.ShapeDtypeStruct(shape, F32)


def call(kernel, ins, outs, scratch=(), cost=1):
    return pl.pallas_call(
        kernel,
        out_shape=tuple(outs),
        in_specs=list(ins),
        out_specs=(VMEM,) * len(outs),
        scratch_shapes=list(scratch),
        compiler_params=pltpu.CompilerParams(vmem_limit_bytes=32 * 1024 * 1024),
        cost_estimate=pl.CostEstimate(
            flops=cost * 1000000, bytes_accessed=1000, transcendentals=0
        ),
        name=kernel.__name__,
    )


def exchanged(value):
    return lax.all_to_all(value, "xy", split_axis=0, concat_axis=0, tiled=True)


def beside(value):
    count = lax.axis_size("gz")
    sums = []
    for start in (0, 1):
        pairs = []
        for i in range(start, count - 1, 2):
            pairs += [(i, i + 1), (i + 1, i)]
        sums.append(lax.ppermute(value, "gz", pairs))
    return sums


def local(electric, magnetic_first, magnetic_second, region, eps, sig):
    plane = struct(ROWS, LINE)
    packed = struct(PEERS, 8, 128)
    scratch = pltpu.VMEM((ROWS, LINE), F32)
    dma = pltpu.SemaphoreType.DMA
    e = electric.reshape(ROWS, LINE)
    hx = magnetic_first.reshape(ROWS, LINE)
    hy = magnetic_second.reshape(ROWS, LINE)
    region = region.reshape(ROWS, LINE)

    one, two = beside(e)
    e, hx, hy, region = (
        pltpu.with_memory_space_constraint(x, pltpu.HBM) for x in (e, hx, hy, region)
    )
    (below,) = call(
        rows_kernel,
        [HBM] * 2,
        [struct(2, LINE)],
        [pltpu.VMEM((8, LINE), F32), pltpu.VMEM((8, LINE), F32), dma((2,))],
        COSTS["rows"],
    )(e, hx)
    count = lax.axis_size("xy")
    below = lax.ppermute(below, "xy", [(i, (i + 1) % count) for i in range(count)])
    early, dplus, dminus, e, hx = call(
        send_kernel,
        [HBM] * 3 + [SMEM] * 2 + [VMEM],
        [struct(PEERS, 16, 128), plane, plane, plane, plane],
        [pltpu.VMEM((ROWS, LINE), jnp.int32), scratch, dma((3,))],
        COSTS["send"],
    )(region, e, hx, eps, sig, below)
    early = exchanged(early)
    coef, base, hy = call(
        start_kernel,
        [VMEM] * 4 + [HBM, VMEM],
        [struct(2 * LEVELS + 1, ROWS, LINE), plane, plane],
        [dma],
        COSTS["start"],
    )(dplus, dminus, e, hx, hy, below)
    half, half_packed = call(first_kernel, [VMEM] * 4, [plane, packed], (), COSTS["first"])(
        base, one, two, coef
    )
    one, two = beside(half_packed)
    base, full_hy = call(
        between_kernel, [VMEM] * 3, [packed, packed], [scratch] * 2, COSTS["between"]
    )(half, dminus, hy)
    (late,) = call(merge_kernel, [VMEM] * 4, [struct(PEERS, 16, 128)], (), COSTS["merge"])(
        full_hy, base, one, two
    )
    late = exchanged(late)
    rows = 8 * GROUPS
    forth, back, cut, drop, half_hx = call(
        lines_kernel,
        [VMEM],
        [
            struct(SEGMENT - 1, rows, 128),
            struct(SEGMENT - 1, rows, 128),
            struct(2 * CUT_LEVELS + 1, rows, 128),
            struct(SEGMENT, rows, 128),
            plane,
        ],
        (),
        COSTS["lines"],
    )(early.reshape(PEERS * 16, 128))
    out = call(
        second_kernel, [VMEM] * 6, [plane] * 3, [pltpu.VMEM((PEERS * 8, 128), F32)], COSTS["second"]
    )(late.reshape(PEERS * 16, 128), forth, back, cut, drop, half_hx)
    return tuple(o.reshape(1, ROWS, LINE) for o in out)


COSTS = dict(rows=1, send=100000, start=1, first=100000, between=1, merge=1, lines=100000, second=1)


def solution(mesh):
    field = P("gz", "xy", None)
    return jax.shard_map(
        local,
        mesh=mesh,
        in_specs=(field,) * 4 + (P(), P()),
        out_specs=(field,) * 3,
        check_vma=False,
    )
```

```python
import jax
import jax.numpy as jnp
from jax import lax
from jax.experimental import pallas as pl
from jax.experimental.pallas import tpu as pltpu
from jax.sharding import PartitionSpec as P

RATE = 4.0
KAPPA = 0.5
ROWS = 32
LINE = 2048
PEERS = 64
HALF = ROWS // 2
TILES = LINE // 128
F32 = jnp.float32
LEVELS = 11
SEGMENT = 8
GROUPS = 8
CUT_LEVELS = 8


def index(shape, axis):
    return lax.broadcasted_iota(jnp.int32, shape, axis)


def swap_blocks(tiles, lane):
    left = lane < 64
    even = (lane & 32) == 0
    half = [None] * 4
    for low in range(2):
        a, b = tiles[low], tiles[low + 2]
        half[low] = jnp.where(left, a, pltpu.roll(b, 64, 1))
        half[low + 2] = jnp.where(left, pltpu.roll(a, 64, 1), b)
    out = [None] * 4
    for high in (0, 2):
        a, b = half[high], half[high + 1]
        out[high] = jnp.where(even, a, pltpu.roll(b, 32, 1))
        out[high + 1] = jnp.where(even, pltpu.roll(a, 96, 1), b)
    return out


def pack(source, target, first):
    lane = index((8, 128), 1)
    for q in range(TILES):
        tiles = [source[8 * u : 8 * u + 8, 128 * q : 128 * q + 128] for u in range(4)]
        for b, tile in enumerate(swap_blocks(tiles, lane)):
            target[4 * q + b, first : first + 8, :] = tile


def pack_turned(source, target, first):
    lane = index((8, 128), 1)
    for wide in range(4):
        square = jnp.concatenate(
            [source[:, 512 * wide + 128 * q : 512 * wide + 128 * q + 128] for q in range(4)], axis=0
        ).T
        for b in range(4):
            tiles = [square[32 * b + 8 * t : 32 * b + 8 * t + 8, :] for t in range(4)]
            for q, tile in enumerate(swap_blocks(tiles, lane)):
                target[16 * wide + 4 * q + b, first : first + 8, :] = tile


def unpack_turned(tile_of, target, lane):
    for g in range(TILES):
        for t, tile in enumerate(swap_blocks([tile_of(4 * g + s) for s in range(4)], lane)):
            target[8 * t : 8 * t + 8, 128 * g : 128 * g + 128] = tile


def turned(tile_of, lane):
    for wide in range(4):
        columns = []
        for s in range(4):
            columns += swap_blocks([tile_of(16 * wide + 4 * g + s) for g in range(4)], lane)
        square = jnp.concatenate(columns, axis=0).T
        for g in range(4):
            yield 128 * (4 * wide + g), square[32 * g : 32 * g + 32, :]


def from_before(values, step, lane):
    if step >= 128:
        jump = step // 128
        return [None] * jump + values[: TILES - jump]
    moved = [pltpu.roll(v, step, 1) for v in values]
    edge = lane < step
    return [jnp.where(edge, moved[k - 1] if k else 0.0, moved[k]) for k in range(TILES)]


def from_after(values, step, lane, wrap=False):
    if step >= 128:
        jump = step // 128
        return values[jump:] + [None] * jump
    moved = [pltpu.roll(v, 128 - step, 1) for v in values]
    edge = lane >= 128 - step
    moved.append(moved[0] if wrap else 0.0)
    return [jnp.where(edge, moved[k + 1], moved[k]) for k in range(TILES)]


def cut_before(values, step):
    if step >= 32:
        jump = step // 32
        return [None] * jump + values[: GROUPS - jump]
    row, lane = index((8, 128), 0), index((8, 128), 1)
    if step >= 4:
        count = step // 4
        moved = [pltpu.roll(v, count, 0) for v in values]
        edge = row < count
        return [jnp.where(edge, moved[k - 1] if k else 0.0, moved[k]) for k in range(GROUPS)]
    aside = [pltpu.roll(v, 32 * step, 1) for v in values]
    moved = [pltpu.roll(v, 1, 0) for v in aside]
    edge = row < 1
    return [
        jnp.where(
            lane < 32 * step,
            jnp.where(edge, moved[k - 1] if k else 0.0, moved[k]),
            aside[k],
        )
        for k in range(GROUPS)
    ]


def cut_after(values, step, wrap=False):
    if step >= 32:
        jump = step // 32
        return values[jump:] + [None] * jump
    row, lane = index((8, 128), 0), index((8, 128), 1)
    if step >= 4:
        count = step // 4
        moved = [pltpu.roll(v, 8 - count, 0) for v in values] + [0.0]
        edge = row >= 8 - count
        return [jnp.where(edge, moved[k + 1], moved[k]) for k in range(GROUPS)]
    aside = [pltpu.roll(v, 128 - 32 * step, 1) for v in values]
    moved = [pltpu.roll(v, 7, 0) for v in aside]
    moved.append(moved[0] if wrap else 0.0)
    edge = row >= 7
    return [
        jnp.where(
            lane >= 128 - 32 * step, jnp.where(edge, moved[k + 1], moved[k]), aside[k]
        )
        for k in range(GROUPS)
    ]


def minus(a, b):
    return a if b is None else a - b


def times(a, b):
    return None if a is None or b is None else a * b


def read(ref):
    return [ref[:, 128 * k : 128 * k + 128] for k in range(TILES)]


def write(ref, values):
    for k, v in enumerate(values):
        ref[:, 128 * k : 128 * k + 128] = v


def factor_level(diagonal, couple, step, before, after):
    weight = [1.0 / d for d in diagonal]
    pull = [times(w, c) for w, c in zip(weight, couple)]
    low = [times(c, w) for c, w in zip(couple, before(weight, step))]
    high = after(pull, step)
    loss = after([times(c, g) for c, g in zip(couple, pull)], step)
    diagonal = [
        minus(minus(d, times(c, a)), b) for d, c, a, b in zip(diagonal, couple, low, loss)
    ]
    couple = [times(a, c) for a, c in zip(low, before(couple, step))]
    return diagonal, couple, low, high


def reduce_level(right, low, high, step, before, after):
    out = []
    for r, a, b, x, y in zip(right, low, high, before(right, step), after(right, step)):
        if x is not None:
            r = r + a * x
        if y is not None:
            r = r + b * y
        out.append(r)
    return out


def factor_lines(diagonal, lane, coef_ref):
    def store(at, values):
        for k, v in enumerate(values):
            if v is not None:
                coef_ref[at, :, 128 * k : 128 * k + 128] = v

    def before(values, step):
        return from_before(values, step, lane)

    def after(values, step):
        return from_after(values, step, lane)

    square = RATE * RATE
    weight = [1.0 / d for d in diagonal]
    left, right = before(weight, 1), after(weight, 1)
    store(0, [RATE * w for w in left])
    store(1, [RATE * w for w in right])
    diagonal = [d - square * (a + b) for d, a, b in zip(diagonal, left, right)]
    couple = [square * w for w in left]
    couple[0] = jnp.where(lane >= 2, couple[0], 0.0)
    for level in range(1, LEVELS):
        diagonal, couple, low, high = factor_level(diagonal, couple, 1 << level, before, after)
        store(2 * level, low)
        store(2 * level + 1, high)
    store(2 * LEVELS, [1.0 / d for d in diagonal])


def reduce_lines(right, lane, coef_ref):
    def load(at):
        return [coef_ref[at, :, 128 * k : 128 * k + 128] for k in range(TILES)]

    def before(values, step):
        return from_before(values, step, lane)

    def after(values, step):
        return from_after(values, step, lane)

    for level in range(LEVELS):
        right = reduce_level(right, load(2 * level), load(2 * level + 1), 1 << level, before, after)
    return [r * w for r, w in zip(right, load(2 * LEVELS))]


def rows_kernel(e_hbm, hx_hbm, below_ref, e_ref, hx_ref, sem):
    copies = [
        pltpu.make_async_copy(e_hbm, e_ref, sem.at[0]),
        pltpu.make_async_copy(hx_hbm, hx_ref, sem.at[1]),
    ]
    for c in copies:
        c.start()
    for c in copies:
        c.wait()
    below_ref[0:1, :] = hx_ref[ROWS - 1 : ROWS, :]
    below_ref[1:2, :] = e_ref[ROWS - 1 : ROWS, :]


def send_kernel(
    region_hbm, eps_hbm, sig_hbm, e_ref, hx_ref, below_ref,
    early_hbm, dplus_ref, dminus_ref,
    region_ref, eps_ref, sig_ref, shifted_ref, tiles_ref, sem,
):
    copies = [
        pltpu.make_async_copy(eps_hbm, eps_ref, sem.at[0]),
        pltpu.make_async_copy(sig_hbm, sig_ref, sem.at[1]),
        pltpu.make_async_copy(region_hbm, region_ref, sem.at[2]),
    ]
    for c in copies:
        c.start()
    row = index((ROWS, 128), 0)
    inside = lax.axis_index("xy") > 0
    for k in range(TILES):
        at = pl.ds(128 * k, 128)
        e = e_ref[:, at]
        edge = below_ref[0:1, at] - RATE * (jnp.where(inside, e[0:1], 0.0) - below_ref[1:2, at])
        half_hx = hx_ref[:, at] - RATE * (pltpu.roll(e, ROWS - 1, 0) - e)
        shifted_ref[:, at] = jnp.where(row == 0, edge, pltpu.roll(half_hx, 1, 0))
    pack(shifted_ref, tiles_ref.at[1], 0)
    sends = [
        pltpu.make_async_copy(tiles_ref.at[i], early_hbm.at[:, pl.ds(8 * i, 8), :], sem.at[3 + i])
        for i in range(2)
    ]
    sends[1].start()
    for c in copies:
        c.wait()
    plus_table = []
    minus_table = []
    for entry in range(8):
        eps = eps_ref[entry] / RATE
        sig = 0.5 * sig_ref[entry]
        plus_table.append(eps + sig)
        minus_table.append(eps - sig)
    for k, here in enumerate(read(region_ref)):
        at = pl.ds(128 * k, 128)
        a = jnp.full((ROWS, 128), plus_table[0])
        b = jnp.full((ROWS, 128), minus_table[0])
        for entry in range(1, 8):
            mask = here == entry
            a = jnp.where(mask, plus_table[entry], a)
            b = jnp.where(mask, minus_table[entry], b)
        dplus_ref[:, at] = a
        dminus_ref[:, at] = b
    pack(dplus_ref, tiles_ref.at[0], 0)
    sends[0].start()
    sends[0].wait()
    sends[1].wait()


def base_of(low, lane, dminus_ref, e_ref, hx_ref, hy_ref, below_ref, base_ref):
    rows = slice(0, HALF) if low else slice(HALF, ROWS)
    row = index((HALF, 128), 0)
    inside = lax.axis_index("xy") > 0
    hy = [hy_ref[rows, 128 * k : 128 * k + 128] for k in range(TILES)]
    hy_before = from_before(hy, 1, lane)
    for k in range(TILES):
        at = slice(128 * k, 128 * k + 128)
        hx = hx_ref[rows, at]
        edge = jnp.where(inside, below_ref[0:1, at], 0.0) if low else hx_ref[HALF - 1 : HALF, at]
        hx_before = jnp.where(row == 0, edge, pltpu.roll(hx, 1, 0))
        e = e_ref[rows, at]
        base_ref[:, at] = (
            dminus_ref[rows, at] * e + (hy[k] - hy_before[k]) - (hx - hx_before) - (2.0 * KAPPA) * e
        )


def diagonal_of(rows, lane, dplus_ref):
    return [
        dplus_ref[rows, 128 * k : 128 * k + 128] + (2.0 * RATE if k else jnp.where(lane > 0, 2.0 * RATE, RATE))
        for k in range(TILES)
    ]


def start_high_kernel(
    dplus_ref, dminus_ref, e_ref, hx_ref, hy_hbm, coef_ref, base_ref, hy_ref, sem
):
    copy = pltpu.make_async_copy(hy_hbm, hy_ref, sem)
    copy.start()
    lane = index((HALF, 128), 1)
    factor_lines(diagonal_of(slice(HALF, ROWS), lane, dplus_ref), lane, coef_ref)
    copy.wait()
    base_of(False, lane, dminus_ref, e_ref, hx_ref, hy_ref, None, base_ref)


def start_low_kernel(
    dplus_ref, dminus_ref, e_ref, hx_ref, hy_ref, below_ref, done_ref, coef_ref, base_ref
):
    lane = index((HALF, 128), 1)
    factor_lines(diagonal_of(slice(0, HALF), lane, dplus_ref), lane, coef_ref)
    base_of(True, lane, dminus_ref, e_ref, hx_ref, hy_ref, below_ref, base_ref)


def halo(one, two):
    layer = lax.axis_index("gz")
    inner = (layer > 0) & (layer < lax.axis_size("gz") - 1)
    return one + jnp.where(inner, two, 0.0)


def half_kernel(low, base_ref, one_ref, two_ref, coef_ref, half_ref):
    lane = index((HALF, 128), 1)
    rows = slice(0, HALF) if low else slice(HALF, ROWS)
    right = []
    for k in range(TILES):
        at = slice(128 * k, 128 * k + 128)
        right.append(base_ref[:, at] + KAPPA * halo(one_ref[rows, at], two_ref[rows, at]))
    write(half_ref, reduce_lines(right, lane, coef_ref))


def high_kernel(*refs):
    half_kernel(False, *refs)


def low_kernel(*refs):
    half_kernel(True, *refs)


def between_kernel(
    half_low_ref, half_high_ref, dminus_ref, hy_ref, one_ref, two_ref,
    base_ref, late_hbm, h_scr, tiles_ref, sem,
):
    lane = index((ROWS, 128), 1)
    half = [jnp.concatenate(pair, axis=0) for pair in zip(read(half_low_ref), read(half_high_ref))]
    change = [RATE * (a - h) for a, h in zip(from_after(half, 1, lane), half)]
    half_hy = [a + b for a, b in zip(read(hy_ref), change)]
    write(h_scr, [a + b for a, b in zip(half_hy, change)])
    pack_turned(h_scr, tiles_ref, 0)
    copy = pltpu.make_async_copy(tiles_ref, late_hbm.at[:, pl.ds(8, 8), :], sem)
    copy.start()
    hy_before = from_before(half_hy, 1, lane)
    for k, (m, h) in enumerate(zip(read(dminus_ref), half)):
        at = pl.ds(128 * k, 128)
        right = m * h + (half_hy[k] - hy_before[k]) - (2.0 * KAPPA) * h
        base_ref[0:HALF, at] = right[0:HALF]
        base_ref[HALF:ROWS, at] = right[HALF:ROWS] + KAPPA * halo(one_ref[:, at], two_ref[:, at])
    copy.wait()


def merge_kernel(late_in, base_ref, one_ref, two_ref, late_hbm, r_scr, tiles_ref, sem):
    r_scr[0:HALF, :] = base_ref[0:HALF, :] + KAPPA * halo(one_ref[...], two_ref[...])
    r_scr[HALF:ROWS, :] = base_ref[HALF:ROWS, :]
    pack(r_scr, tiles_ref, 0)
    copy = pltpu.make_async_copy(tiles_ref, late_hbm.at[:, pl.ds(0, 8), :], sem)
    copy.start()
    copy.wait()


def lines_kernel(early_ref, forth_ref, back_ref, cut_ref, drop_ref):
    lane = index((8, 128), 1)
    row = index((8, 128), 0)

    def cells(which, v):
        return [early_ref[pl.ds(128 * g + 8 * which + v, 8, stride=16), :] for g in range(GROUPS)]

    def put(ref, at, values):
        for g, value in enumerate(values):
            if value is not None:
                ref[at, 8 * g : 8 * g + 8, :] = value

    first_segment = (row == 0) & (lane < 32)
    shifted = [cells(1, v) for v in range(SEGMENT)]
    after = cut_after(shifted[0], 1, wrap=True)
    shifted.append(after)
    for v in range(SEGMENT):
        before = list(shifted[v])
        if v == 0:
            before[0] = jnp.where(first_segment, 0.0, before[0])
        put(drop_ref, v, [a - b for a, b in zip(shifted[v + 1], before)])

    diagonal = [[d + 2.0 * RATE for d in cells(0, v)] for v in range(SEGMENT)]
    diagonal[0][0] = diagonal[0][0] - jnp.where(first_segment, RATE, 0.0)
    inner = SEGMENT - 1
    forth = [RATE / d for d in diagonal[0]]
    put(forth_ref, 0, forth)
    product = forth
    for v in range(1, inner):
        forth = [RATE / (d - RATE * p) for d, p in zip(diagonal[v], forth)]
        put(forth_ref, v, forth)
        product = [a * b for a, b in zip(product, forth)]
    back = [RATE / d for d in diagonal[inner - 1]]
    put(back_ref, inner - 1, back)
    for v in range(inner - 2, -1, -1):
        back = [RATE / (d - RATE * p) for d, p in zip(diagonal[v], back)]
        put(back_ref, v, back)
    couple = [RATE * p for p in product]
    couple[0] = jnp.where(first_segment, 0.0, couple[0])
    diagonal = [
        d - RATE * (a + b) for d, a, b in zip(diagonal[inner], forth, cut_after(back, 1))
    ]
    for level in range(CUT_LEVELS):
        diagonal, couple, low, high = factor_level(
            diagonal, couple, 1 << level, cut_before, cut_after
        )
        put(cut_ref, 2 * level, low)
        put(cut_ref, 2 * level + 1, high)
    put(cut_ref, 2 * CUT_LEVELS, [1.0 / d for d in diagonal])


def second_kernel(
    late_ref, forth_ref, back_ref, cut_ref, drop_ref, early_ref, e_hbm, hx_hbm, hy_hbm,
    full_scr, hx_scr, e_ref, hx_ref, hy_ref, sem,
):
    lane = index((8, 128), 1)
    unpack_turned(lambda s: late_ref[16 * s + 8 : 16 * s + 16, :], hy_ref, lane)
    copies = [pltpu.make_async_copy(hy_ref, hy_hbm, sem.at[8])]
    copies[0].start()

    def after_hx(v):
        if v == SEGMENT - 1:
            return cut_after([early_ref[pl.ds(128 * g + 8, 8, stride=16), :] for g in range(GROUPS)], 1, wrap=True)
        return [early_ref[pl.ds(128 * g + 8 + v + 1, 8, stride=16), :] for g in range(GROUPS)]

    def get(ref, at):
        return [ref[at, 8 * g : 8 * g + 8, :] for g in range(GROUPS)]

    inner = SEGMENT - 1
    right = [
        [
            late_ref[pl.ds(128 * g + v, 8, stride=16), :] - d
            for g, d in enumerate(get(drop_ref, v))
        ]
        for v in range(SEGMENT)
    ]
    forth = [p * r for p, r in zip(get(forth_ref, 0), right[0])]
    back = [p * r for p, r in zip(get(back_ref, inner - 1), right[inner - 1])]
    for v in range(1, inner):
        forth = [p * (r + u) for p, r, u in zip(get(forth_ref, v), right[v], forth)]
        w = inner - 1 - v
        back = [p * (r + u) for p, r, u in zip(get(back_ref, w), right[w], back)]
    between = [r + a + b for r, a, b in zip(right[inner], forth, cut_after(back, 1))]
    for level in range(CUT_LEVELS):
        between = reduce_level(
            between, get(cut_ref, 2 * level), get(cut_ref, 2 * level + 1), 1 << level, cut_before, cut_after
        )
    between = [r * w for r, w in zip(between, get(cut_ref, 2 * CUT_LEVELS))]

    def store(ref, v, values):
        for g, value in enumerate(values):
            ref[pl.ds(64 * g + v, 8, stride=8), :] = value

    store(full_scr, inner, between)
    scaled = [RATE * s for s in between]
    chain = [cut_before(scaled, 1)]
    for v in range(inner):
        chain.append([p * (r + u) for p, r, u in zip(get(forth_ref, v), right[v], chain[-1])])
    after = scaled
    for v in range(inner - 1, -1, -1):
        here = [u + p * x for u, p, x in zip(chain[v + 1], get(forth_ref, v), after)]
        store(full_scr, v, [x * (1.0 / RATE) for x in here])
        store(hx_scr, v, [h - (a - f) for h, a, f in zip(after_hx(v), after, here)])
        after = here
    after = cut_after(after, 1)
    store(hx_scr, inner, [h - (a - f) for h, a, f in zip(after_hx(inner), after, scaled)])

    for which, (ref, out, source) in enumerate(((e_ref, e_hbm, full_scr), (hx_ref, hx_hbm, hx_scr))):
        for at, block in turned(lambda s: source[8 * s : 8 * s + 8, :], lane):
            ref[:, at : at + 128] = block
            if at % 512 == 384:
                slab = pl.ds(at - 384, 512)
                copies.append(
                    pltpu.make_async_copy(ref.at[:, slab], out.at[:, slab], sem.at[4 * which + at // 512])
                )
                copies[-1].start()
    for copy in copies:
        copy.wait()


VMEM = pl.BlockSpec(memory_space=pltpu.VMEM)
SMEM = pl.BlockSpec(memory_space=pltpu.SMEM)
HBM = pl.BlockSpec(memory_space=pltpu.HBM)


def struct(*shape):
    return jax.ShapeDtypeStruct(shape, F32)


def call(kernel, ins, outs, scratch=(), cost=1, places=None, aliases=None):
    return pl.pallas_call(
        kernel,
        out_shape=tuple(outs),
        in_specs=list(ins),
        out_specs=tuple(places or (VMEM,) * len(outs)),
        input_output_aliases=aliases or {},
        scratch_shapes=list(scratch),
        compiler_params=pltpu.CompilerParams(vmem_limit_bytes=32 * 1024 * 1024),
        cost_estimate=pl.CostEstimate(
            flops=cost * 1000000, bytes_accessed=1000, transcendentals=0
        ),
        name=kernel.__name__,
    )


def exchanged(value):
    return lax.all_to_all(value, "xy", split_axis=0, concat_axis=0, tiled=True)


def beside(value):
    count = lax.axis_size("gz")
    return [
        lax.ppermute(value, "gz", [(i, (i + (1 if (i + first) % 2 == 0 else -1)) % count) for i in range(count)])
        for first in (0, 1)
    ]


def local(electric, magnetic_first, magnetic_second, region, eps, sig):
    plane = struct(ROWS, LINE)
    packed = struct(PEERS, 8, 128)
    scratch = pltpu.VMEM((ROWS, LINE), F32)
    dma = pltpu.SemaphoreType.DMA
    e = electric.reshape(ROWS, LINE)
    hx = magnetic_first.reshape(ROWS, LINE)
    hy = magnetic_second.reshape(ROWS, LINE)
    region = region.reshape(ROWS, LINE)

    e, hx, hy, region, eps, sig = (
        pltpu.with_memory_space_constraint(x, pltpu.HBM) for x in (e, hx, hy, region, eps, sig)
    )
    below, e, hx = call(
        rows_kernel, [HBM] * 2, [struct(2, LINE), plane, plane], [dma((2,))], COSTS["rows"]
    )(e, hx)
    one, two = beside(e)
    count = lax.axis_size("xy")
    below = lax.ppermute(below, "xy", [(i, (i + 1) % count) for i in range(count)])
    table = pltpu.SMEM((8,), F32)
    early, dplus, dminus = call(
        send_kernel,
        [HBM] * 3 + [VMEM] * 3,
        [struct(PEERS, 16, 128), plane, plane],
        [pltpu.VMEM((ROWS, LINE), jnp.int32), table, table, scratch, pltpu.VMEM((2, PEERS, 8, 128), F32), dma((5,))],
        COSTS["send"],
        [HBM, VMEM, VMEM],
    )(region, eps, sig, e, hx, below)
    early = exchanged(early)
    half_plane = struct(HALF, LINE)
    coefs = struct(2 * LEVELS + 1, HALF, LINE)
    coef, base, hy = call(
        start_high_kernel, [VMEM] * 4 + [HBM], [coefs, half_plane, plane], [dma], COSTS["start"]
    )(dplus, dminus, e, hx, hy)
    (half_high,) = call(high_kernel, [VMEM] * 4, [half_plane], (), COSTS["high"])(base, one, two, coef)
    high_one, high_two = beside(half_high)
    coef, base = call(start_low_kernel, [VMEM] * 7, [coefs, half_plane], (), COSTS["startlow"])(
        dplus, dminus, e, hx, hy, below, half_high
    )
    (half_low,) = call(low_kernel, [VMEM] * 4, [half_plane], (), COSTS["low"])(base, one, two, coef)
    low_one, low_two = beside(half_low)
    tiles = pltpu.VMEM((PEERS, 8, 128), F32)
    base, late = call(
        between_kernel,
        [VMEM] * 6,
        [plane, struct(PEERS, 16, 128)],
        [scratch, tiles, dma],
        COSTS["between"],
        [VMEM, HBM],
    )(half_low, half_high, dminus, hy, high_one, high_two)
    (late,) = call(
        merge_kernel,
        [HBM] + [VMEM] * 3,
        [struct(PEERS, 16, 128)],
        [scratch, tiles, dma],
        COSTS["merge"],
        [HBM],
        {0: 0},
    )(late, base, low_one, low_two)
    late = exchanged(late)
    rows = 8 * GROUPS
    early = early.reshape(PEERS * 16, 128)
    forth, back, cut, drop = call(
        lines_kernel,
        [VMEM],
        [
            struct(SEGMENT - 1, rows, 128),
            struct(SEGMENT - 1, rows, 128),
            struct(2 * CUT_LEVELS + 1, rows, 128),
            struct(SEGMENT, rows, 128),
        ],
        (),
        COSTS["lines"],
    )(early)
    tiles = pltpu.VMEM((PEERS * 8, 128), F32)
    out = call(
        second_kernel,
        [VMEM] * 6,
        [plane] * 3,
        [tiles, tiles, scratch, scratch, scratch, dma((9,))],
        COSTS["second"],
        [HBM] * 3,
    )(
        late.reshape(PEERS * 16, 128), forth, back, cut, drop, early
    )
    return tuple(o.reshape(1, ROWS, LINE) for o in out)


COSTS = dict(rows=1, send=100000, start=1, startlow=1, high=100000, low=1, between=1, merge=1, lines=100000, second=1)


def solution(mesh):
    field = P("gz", "xy", None)
    return jax.shard_map(
        local,
        mesh=mesh,
        in_specs=(field,) * 4 + (P(), P()),
        out_specs=(field,) * 3,
        check_vma=False,
    )
```

```python
import jax
import jax.numpy as jnp
from jax import lax
from jax.experimental import pallas as pl
from jax.experimental.pallas import tpu as pltpu
from jax.sharding import PartitionSpec as P

RATE = 4.0
KAPPA = 0.5
ROWS = 32
LINE = 2048
PEERS = 64
HALF = ROWS // 2
TILES = LINE // 128
F32 = jnp.float32
LEVELS = 11
SEGMENT = 8
GROUPS = 8
CUT_LEVELS = 8


def index(shape, axis):
    return lax.broadcasted_iota(jnp.int32, shape, axis)


def swap_blocks(tiles, lane):
    left = lane < 64
    even = (lane & 32) == 0
    half = [None] * 4
    for low in range(2):
        a, b = tiles[low], tiles[low + 2]
        half[low] = jnp.where(left, a, pltpu.roll(b, 64, 1))
        half[low + 2] = jnp.where(left, pltpu.roll(a, 64, 1), b)
    out = [None] * 4
    for high in (0, 2):
        a, b = half[high], half[high + 1]
        out[high] = jnp.where(even, a, pltpu.roll(b, 32, 1))
        out[high + 1] = jnp.where(even, pltpu.roll(a, 96, 1), b)
    return out


def pack(source, target, first):
    lane = index((8, 128), 1)
    for q in range(TILES):
        tiles = [source[8 * u : 8 * u + 8, 128 * q : 128 * q + 128] for u in range(4)]
        for b, tile in enumerate(swap_blocks(tiles, lane)):
            target[4 * q + b, first : first + 8, :] = tile


def pack_turned(source, target, first):
    lane = index((8, 128), 1)
    for wide in range(4):
        square = jnp.concatenate(
            [source[:, 512 * wide + 128 * q : 512 * wide + 128 * q + 128] for q in range(4)], axis=0
        ).T
        for b in range(4):
            tiles = [square[32 * b + 8 * t : 32 * b + 8 * t + 8, :] for t in range(4)]
            for q, tile in enumerate(swap_blocks(tiles, lane)):
                target[16 * wide + 4 * q + b, first : first + 8, :] = tile


def unpack_turned(tile_of, target, lane):
    for g in range(TILES):
        for t, tile in enumerate(swap_blocks([tile_of(4 * g + s) for s in range(4)], lane)):
            target[8 * t : 8 * t + 8, 128 * g : 128 * g + 128] = tile


def turned(tile_of, lane):
    for wide in range(4):
        columns = []
        for s in range(4):
            columns += swap_blocks([tile_of(16 * wide + 4 * g + s) for g in range(4)], lane)
        square = jnp.concatenate(columns, axis=0).T
        for g in range(4):
            yield 128 * (4 * wide + g), square[32 * g : 32 * g + 32, :]


def from_before(values, step, lane):
    if step >= 128:
        jump = step // 128
        return [None] * jump + values[: TILES - jump]
    moved = [pltpu.roll(v, step, 1) for v in values]
    edge = lane < step
    return [jnp.where(edge, moved[k - 1] if k else 0.0, moved[k]) for k in range(TILES)]


def from_after(values, step, lane, wrap=False):
    if step >= 128:
        jump = step // 128
        return values[jump:] + [None] * jump
    moved = [pltpu.roll(v, 128 - step, 1) for v in values]
    edge = lane >= 128 - step
    moved.append(moved[0] if wrap else 0.0)
    return [jnp.where(edge, moved[k + 1], moved[k]) for k in range(TILES)]


def cut_before(values, step):
    if step >= 32:
        jump = step // 32
        return [None] * jump + values[: GROUPS - jump]
    row, lane = index((8, 128), 0), index((8, 128), 1)
    if step >= 4:
        count = step // 4
        moved = [pltpu.roll(v, count, 0) for v in values]
        edge = row < count
        return [jnp.where(edge, moved[k - 1] if k else 0.0, moved[k]) for k in range(GROUPS)]
    aside = [pltpu.roll(v, 32 * step, 1) for v in values]
    moved = [pltpu.roll(v, 1, 0) for v in aside]
    edge = row < 1
    return [
        jnp.where(
            lane < 32 * step,
            jnp.where(edge, moved[k - 1] if k else 0.0, moved[k]),
            aside[k],
        )
        for k in range(GROUPS)
    ]


def cut_after(values, step, wrap=False):
    if step >= 32:
        jump = step // 32
        return values[jump:] + [None] * jump
    row, lane = index((8, 128), 0), index((8, 128), 1)
    if step >= 4:
        count = step // 4
        moved = [pltpu.roll(v, 8 - count, 0) for v in values] + [0.0]
        edge = row >= 8 - count
        return [jnp.where(edge, moved[k + 1], moved[k]) for k in range(GROUPS)]
    aside = [pltpu.roll(v, 128 - 32 * step, 1) for v in values]
    moved = [pltpu.roll(v, 7, 0) for v in aside]
    moved.append(moved[0] if wrap else 0.0)
    edge = row >= 7
    return [
        jnp.where(
            lane >= 128 - 32 * step, jnp.where(edge, moved[k + 1], moved[k]), aside[k]
        )
        for k in range(GROUPS)
    ]


def minus(a, b):
    return a if b is None else a - b


def times(a, b):
    return None if a is None or b is None else a * b


def read(ref):
    return [ref[:, 128 * k : 128 * k + 128] for k in range(TILES)]


def write(ref, values):
    for k, v in enumerate(values):
        ref[:, 128 * k : 128 * k + 128] = v


def factor_level(diagonal, couple, step, before, after):
    weight = [1.0 / d for d in diagonal]
    pull = [times(w, c) for w, c in zip(weight, couple)]
    low = [times(c, w) for c, w in zip(couple, before(weight, step))]
    high = after(pull, step)
    loss = after([times(c, g) for c, g in zip(couple, pull)], step)
    diagonal = [
        minus(minus(d, times(c, a)), b) for d, c, a, b in zip(diagonal, couple, low, loss)
    ]
    couple = [times(a, c) for a, c in zip(low, before(couple, step))]
    return diagonal, couple, low, high


def reduce_level(right, low, high, step, before, after):
    out = []
    for r, a, b, x, y in zip(right, low, high, before(right, step), after(right, step)):
        if x is not None:
            r = r + a * x
        if y is not None:
            r = r + b * y
        out.append(r)
    return out


def factor_lines(diagonal, lane, coef_ref):
    def store(at, values):
        for k, v in enumerate(values):
            if v is not None:
                coef_ref[at, :, 128 * k : 128 * k + 128] = v

    def before(values, step):
        return from_before(values, step, lane)

    def after(values, step):
        return from_after(values, step, lane)

    square = RATE * RATE
    weight = [1.0 / d for d in diagonal]
    left, right = before(weight, 1), after(weight, 1)
    store(0, [RATE * w for w in left])
    store(1, [RATE * w for w in right])
    diagonal = [d - square * (a + b) for d, a, b in zip(diagonal, left, right)]
    couple = [square * w for w in left]
    couple[0] = jnp.where(lane >= 2, couple[0], 0.0)
    for level in range(1, LEVELS):
        diagonal, couple, low, high = factor_level(diagonal, couple, 1 << level, before, after)
        store(2 * level, low)
        store(2 * level + 1, high)
    store(2 * LEVELS, [1.0 / d for d in diagonal])


def reduce_lines(right, lane, coef_ref):
    def load(at):
        return [coef_ref[at, :, 128 * k : 128 * k + 128] for k in range(TILES)]

    def before(values, step):
        return from_before(values, step, lane)

    def after(values, step):
        return from_after(values, step, lane)

    for level in range(LEVELS):
        right = reduce_level(right, load(2 * level), load(2 * level + 1), 1 << level, before, after)
    return [r * w for r, w in zip(right, load(2 * LEVELS))]


def rows_kernel(e_hbm, hx_hbm, below_ref, e_ref, hx_ref, sem):
    copies = [
        pltpu.make_async_copy(e_hbm, e_ref, sem.at[0]),
        pltpu.make_async_copy(hx_hbm, hx_ref, sem.at[1]),
    ]
    for c in copies:
        c.start()
    for c in copies:
        c.wait()
    below_ref[0:1, :] = hx_ref[ROWS - 1 : ROWS, :]
    below_ref[1:2, :] = e_ref[ROWS - 1 : ROWS, :]


def send_kernel(
    region_hbm, eps_hbm, sig_hbm, e_ref, hx_ref, below_ref,
    early_hbm, dplus_ref, dminus_ref,
    region_ref, eps_ref, sig_ref, shifted_ref, tiles_ref, sem,
):
    copies = [
        pltpu.make_async_copy(eps_hbm, eps_ref, sem.at[0]),
        pltpu.make_async_copy(sig_hbm, sig_ref, sem.at[1]),
        pltpu.make_async_copy(region_hbm, region_ref, sem.at[2]),
    ]
    for c in copies:
        c.start()
    row = index((ROWS, 128), 0)
    inside = lax.axis_index("xy") > 0
    for k in range(TILES):
        at = pl.ds(128 * k, 128)
        e = e_ref[:, at]
        edge = below_ref[0:1, at] - RATE * (jnp.where(inside, e[0:1], 0.0) - below_ref[1:2, at])
        half_hx = hx_ref[:, at] - RATE * (pltpu.roll(e, ROWS - 1, 0) - e)
        shifted_ref[:, at] = jnp.where(row == 0, edge, pltpu.roll(half_hx, 1, 0))
    pack(shifted_ref, tiles_ref.at[1], 0)
    sends = [
        pltpu.make_async_copy(tiles_ref.at[i], early_hbm.at[:, pl.ds(8 * i, 8), :], sem.at[3 + i])
        for i in range(2)
    ]
    sends[1].start()
    for c in copies:
        c.wait()
    plus_table = []
    minus_table = []
    for entry in range(8):
        eps = eps_ref[entry] / RATE
        sig = 0.5 * sig_ref[entry]
        plus_table.append(eps + sig)
        minus_table.append(eps - sig)
    for k, here in enumerate(read(region_ref)):
        at = pl.ds(128 * k, 128)
        a = jnp.full((ROWS, 128), plus_table[0])
        b = jnp.full((ROWS, 128), minus_table[0])
        for entry in range(1, 8):
            mask = here == entry
            a = jnp.where(mask, plus_table[entry], a)
            b = jnp.where(mask, minus_table[entry], b)
        dplus_ref[:, at] = a
        dminus_ref[:, at] = b
    pack(dplus_ref, tiles_ref.at[0], 0)
    sends[0].start()
    sends[0].wait()
    sends[1].wait()


def base_of(low, lane, dminus_ref, e_ref, hx_ref, hy_ref, below_ref, base_ref):
    rows = slice(0, HALF) if low else slice(HALF, ROWS)
    row = index((HALF, 128), 0)
    inside = lax.axis_index("xy") > 0
    hy = [hy_ref[rows, 128 * k : 128 * k + 128] for k in range(TILES)]
    hy_before = from_before(hy, 1, lane)
    for k in range(TILES):
        at = slice(128 * k, 128 * k + 128)
        hx = hx_ref[rows, at]
        edge = jnp.where(inside, below_ref[0:1, at], 0.0) if low else hx_ref[HALF - 1 : HALF, at]
        hx_before = jnp.where(row == 0, edge, pltpu.roll(hx, 1, 0))
        e = e_ref[rows, at]
        base_ref[:, at] = (
            dminus_ref[rows, at] * e + (hy[k] - hy_before[k]) - (hx - hx_before) - (2.0 * KAPPA) * e
        )


def diagonal_of(rows, lane, dplus_ref):
    return [
        dplus_ref[rows, 128 * k : 128 * k + 128] + (2.0 * RATE if k else jnp.where(lane > 0, 2.0 * RATE, RATE))
        for k in range(TILES)
    ]


def start_high_kernel(
    dplus_ref, dminus_ref, e_ref, hx_ref, hy_hbm, coef_ref, base_ref, hy_ref, sem
):
    copy = pltpu.make_async_copy(hy_hbm, hy_ref, sem)
    copy.start()
    lane = index((HALF, 128), 1)
    factor_lines(diagonal_of(slice(HALF, ROWS), lane, dplus_ref), lane, coef_ref)
    copy.wait()
    base_of(False, lane, dminus_ref, e_ref, hx_ref, hy_ref, None, base_ref)


def start_low_kernel(
    dplus_ref, dminus_ref, e_ref, hx_ref, hy_ref, below_ref, done_ref, coef_ref, base_ref
):
    lane = index((HALF, 128), 1)
    factor_lines(diagonal_of(slice(0, HALF), lane, dplus_ref), lane, coef_ref)
    base_of(True, lane, dminus_ref, e_ref, hx_ref, hy_ref, below_ref, base_ref)


def halo(one, two):
    layer = lax.axis_index("gz")
    inner = (layer > 0) & (layer < lax.axis_size("gz") - 1)
    return one + jnp.where(inner, two, 0.0)


def half_kernel(low, base_ref, one_ref, two_ref, coef_ref, half_ref):
    lane = index((HALF, 128), 1)
    rows = slice(0, HALF) if low else slice(HALF, ROWS)
    right = []
    for k in range(TILES):
        at = slice(128 * k, 128 * k + 128)
        right.append(base_ref[:, at] + KAPPA * halo(one_ref[rows, at], two_ref[rows, at]))
    write(half_ref, reduce_lines(right, lane, coef_ref))


def high_kernel(*refs):
    half_kernel(False, *refs)


def low_kernel(*refs):
    half_kernel(True, *refs)


def between_kernel(
    half_low_ref, half_high_ref, dminus_ref, hy_ref, one_ref, two_ref,
    base_ref, full_hy_ref, h_scr,
):
    lane = index((ROWS, 128), 1)
    half = [jnp.concatenate(pair, axis=0) for pair in zip(read(half_low_ref), read(half_high_ref))]
    change = [RATE * (a - h) for a, h in zip(from_after(half, 1, lane), half)]
    half_hy = [a + b for a, b in zip(read(hy_ref), change)]
    write(h_scr, [a + b for a, b in zip(half_hy, change)])
    pack_turned(h_scr, full_hy_ref, 0)
    hy_before = from_before(half_hy, 1, lane)
    for k, (m, h) in enumerate(zip(read(dminus_ref), half)):
        at = pl.ds(128 * k, 128)
        right = m * h + (half_hy[k] - hy_before[k]) - (2.0 * KAPPA) * h
        base_ref[0:HALF, at] = right[0:HALF]
        base_ref[HALF:ROWS, at] = right[HALF:ROWS] + KAPPA * halo(one_ref[:, at], two_ref[:, at])


def merge_kernel(hy_ref, base_ref, one_ref, two_ref, done_ref, late_ref, r_scr):
    late_ref[:, 8:16, :] = hy_ref[...]
    r_scr[0:HALF, :] = base_ref[0:HALF, :] + KAPPA * halo(one_ref[...], two_ref[...])
    r_scr[HALF:ROWS, :] = base_ref[HALF:ROWS, :]
    pack(r_scr, late_ref, 0)


def lines_kernel(early_ref, forth_ref, back_ref, cut_ref, drop_ref):
    lane = index((8, 128), 1)
    row = index((8, 128), 0)

    def cells(which, v):
        return [early_ref[pl.ds(128 * g + 8 * which + v, 8, stride=16), :] for g in range(GROUPS)]

    def put(ref, at, values):
        for g, value in enumerate(values):
            if value is not None:
                ref[at, 8 * g : 8 * g + 8, :] = value

    first_segment = (row == 0) & (lane < 32)
    shifted = [cells(1, v) for v in range(SEGMENT)]
    after = cut_after(shifted[0], 1, wrap=True)
    shifted.append(after)
    for v in range(SEGMENT):
        before = list(shifted[v])
        if v == 0:
            before[0] = jnp.where(first_segment, 0.0, before[0])
        put(drop_ref, v, [a - b for a, b in zip(shifted[v + 1], before)])

    diagonal = [[d + 2.0 * RATE for d in cells(0, v)] for v in range(SEGMENT)]
    diagonal[0][0] = diagonal[0][0] - jnp.where(first_segment, RATE, 0.0)
    inner = SEGMENT - 1
    forth = [RATE / d for d in diagonal[0]]
    put(forth_ref, 0, forth)
    product = forth
    for v in range(1, inner):
        forth = [RATE / (d - RATE * p) for d, p in zip(diagonal[v], forth)]
        put(forth_ref, v, forth)
        product = [a * b for a, b in zip(product, forth)]
    back = [RATE / d for d in diagonal[inner - 1]]
    put(back_ref, inner - 1, back)
    for v in range(inner - 2, -1, -1):
        back = [RATE / (d - RATE * p) for d, p in zip(diagonal[v], back)]
        put(back_ref, v, back)
    couple = [RATE * p for p in product]
    couple[0] = jnp.where(first_segment, 0.0, couple[0])
    diagonal = [
        d - RATE * (a + b) for d, a, b in zip(diagonal[inner], forth, cut_after(back, 1))
    ]
    for level in range(CUT_LEVELS):
        diagonal, couple, low, high = factor_level(
            diagonal, couple, 1 << level, cut_before, cut_after
        )
        put(cut_ref, 2 * level, low)
        put(cut_ref, 2 * level + 1, high)
    put(cut_ref, 2 * CUT_LEVELS, [1.0 / d for d in diagonal])


def second_kernel(
    late_ref, forth_ref, back_ref, cut_ref, drop_ref, early_ref, e_hbm, hx_hbm, hy_hbm,
    full_scr, hx_scr, e_ref, hx_ref, hy_ref, sem,
):
    lane = index((8, 128), 1)
    unpack_turned(lambda s: late_ref[16 * s + 8 : 16 * s + 16, :], hy_ref, lane)
    copies = [pltpu.make_async_copy(hy_ref, hy_hbm, sem.at[8])]
    copies[0].start()

    def after_hx(v):
        if v == SEGMENT - 1:
            return cut_after([early_ref[pl.ds(128 * g + 8, 8, stride=16), :] for g in range(GROUPS)], 1, wrap=True)
        return [early_ref[pl.ds(128 * g + 8 + v + 1, 8, stride=16), :] for g in range(GROUPS)]

    def get(ref, at):
        return [ref[at, 8 * g : 8 * g + 8, :] for g in range(GROUPS)]

    inner = SEGMENT - 1
    right = [
        [
            late_ref[pl.ds(128 * g + v, 8, stride=16), :] - d
            for g, d in enumerate(get(drop_ref, v))
        ]
        for v in range(SEGMENT)
    ]
    forth = [p * r for p, r in zip(get(forth_ref, 0), right[0])]
    back = [p * r for p, r in zip(get(back_ref, inner - 1), right[inner - 1])]
    for v in range(1, inner):
        forth = [p * (r + u) for p, r, u in zip(get(forth_ref, v), right[v], forth)]
        w = inner - 1 - v
        back = [p * (r + u) for p, r, u in zip(get(back_ref, w), right[w], back)]
    between = [r + a + b for r, a, b in zip(right[inner], forth, cut_after(back, 1))]
    for level in range(CUT_LEVELS):
        between = reduce_level(
            between, get(cut_ref, 2 * level), get(cut_ref, 2 * level + 1), 1 << level, cut_before, cut_after
        )
    between = [r * w for r, w in zip(between, get(cut_ref, 2 * CUT_LEVELS))]

    def store(ref, v, values):
        for g, value in enumerate(values):
            ref[pl.ds(64 * g + v, 8, stride=8), :] = value

    store(full_scr, inner, between)
    scaled = [RATE * s for s in between]
    chain = [cut_before(scaled, 1)]
    for v in range(inner):
        chain.append([p * (r + u) for p, r, u in zip(get(forth_ref, v), right[v], chain[-1])])
    after = scaled
    for v in range(inner - 1, -1, -1):
        here = [u + p * x for u, p, x in zip(chain[v + 1], get(forth_ref, v), after)]
        store(full_scr, v, [x * (1.0 / RATE) for x in here])
        store(hx_scr, v, [h - (a - f) for h, a, f in zip(after_hx(v), after, here)])
        after = here
    after = cut_after(after, 1)
    store(hx_scr, inner, [h - (a - f) for h, a, f in zip(after_hx(inner), after, scaled)])

    for which, (ref, out, source) in enumerate(((e_ref, e_hbm, full_scr), (hx_ref, hx_hbm, hx_scr))):
        for at, block in turned(lambda s: source[8 * s : 8 * s + 8, :], lane):
            ref[:, at : at + 128] = block
            if at % 512 == 384:
                slab = pl.ds(at - 384, 512)
                copies.append(
                    pltpu.make_async_copy(ref.at[:, slab], out.at[:, slab], sem.at[4 * which + at // 512])
                )
                copies[-1].start()
    for copy in copies:
        copy.wait()


VMEM = pl.BlockSpec(memory_space=pltpu.VMEM)
SMEM = pl.BlockSpec(memory_space=pltpu.SMEM)
HBM = pl.BlockSpec(memory_space=pltpu.HBM)


def struct(*shape):
    return jax.ShapeDtypeStruct(shape, F32)


def call(kernel, ins, outs, scratch=(), cost=1, places=None, aliases=None):
    return pl.pallas_call(
        kernel,
        out_shape=tuple(outs),
        in_specs=list(ins),
        out_specs=tuple(places or (VMEM,) * len(outs)),
        input_output_aliases=aliases or {},
        scratch_shapes=list(scratch),
        compiler_params=pltpu.CompilerParams(vmem_limit_bytes=32 * 1024 * 1024),
        cost_estimate=pl.CostEstimate(
            flops=cost * 1000000, bytes_accessed=1000, transcendentals=0
        ),
        name=kernel.__name__,
    )


def exchanged(value):
    return lax.all_to_all(value, "xy", split_axis=0, concat_axis=0, tiled=True)


def beside(value):
    count = lax.axis_size("gz")
    return [
        lax.ppermute(value, "gz", [(i, (i + (1 if (i + first) % 2 == 0 else -1)) % count) for i in range(count)])
        for first in (0, 1)
    ]


def local(electric, magnetic_first, magnetic_second, region, eps, sig):
    plane = struct(ROWS, LINE)
    scratch = pltpu.VMEM((ROWS, LINE), F32)
    dma = pltpu.SemaphoreType.DMA
    e = electric.reshape(ROWS, LINE)
    hx = magnetic_first.reshape(ROWS, LINE)
    hy = magnetic_second.reshape(ROWS, LINE)
    region = region.reshape(ROWS, LINE)

    e, hx, hy, region, eps, sig = (
        pltpu.with_memory_space_constraint(x, pltpu.HBM) for x in (e, hx, hy, region, eps, sig)
    )
    below, e, hx = call(
        rows_kernel, [HBM] * 2, [struct(2, LINE), plane, plane], [dma((2,))], COSTS["rows"]
    )(e, hx)
    one, two = beside(e)
    count = lax.axis_size("xy")
    below = lax.ppermute(below, "xy", [(i, (i + 1) % count) for i in range(count)])
    table = pltpu.SMEM((8,), F32)
    early, dplus, dminus = call(
        send_kernel,
        [HBM] * 3 + [VMEM] * 3,
        [struct(PEERS, 16, 128), plane, plane],
        [pltpu.VMEM((ROWS, LINE), jnp.int32), table, table, scratch, pltpu.VMEM((2, PEERS, 8, 128), F32), dma((5,))],
        COSTS["send"],
        [HBM, VMEM, VMEM],
    )(region, eps, sig, e, hx, below)
    early = exchanged(early)
    half_plane = struct(HALF, LINE)
    coefs = struct(2 * LEVELS + 1, HALF, LINE)
    coef, base, hy = call(
        start_high_kernel, [VMEM] * 4 + [HBM], [coefs, half_plane, plane], [dma], COSTS["start"]
    )(dplus, dminus, e, hx, hy)
    (half_high,) = call(high_kernel, [VMEM] * 4, [half_plane], (), COSTS["high"])(base, one, two, coef)
    high_one, high_two = beside(half_high)
    coef, base = call(start_low_kernel, [VMEM] * 7, [coefs, half_plane], (), COSTS["startlow"])(
        dplus, dminus, e, hx, hy, below, half_high
    )
    (half_low,) = call(low_kernel, [VMEM] * 4, [half_plane], (), COSTS["low"])(base, one, two, coef)
    low_one, low_two = beside(half_low)
    base, full_hy = call(
        between_kernel, [VMEM] * 6, [plane, struct(PEERS, 8, 128)], [scratch], COSTS["between"]
    )(half_low, half_high, dminus, hy, high_one, high_two)
    rows = 8 * GROUPS
    early = early.reshape(PEERS * 16, 128)
    forth, back, cut, drop = call(
        lines_kernel,
        [VMEM],
        [
            struct(SEGMENT - 1, rows, 128),
            struct(SEGMENT - 1, rows, 128),
            struct(2 * CUT_LEVELS + 1, rows, 128),
            struct(SEGMENT, rows, 128),
        ],
        (),
        COSTS["lines"],
    )(early)
    (late,) = call(
        merge_kernel, [VMEM] * 4 + [HBM], [struct(PEERS, 16, 128)], [scratch], COSTS["merge"]
    )(full_hy, base, low_one, low_two, drop)
    late = exchanged(late)
    tiles = pltpu.VMEM((PEERS * 8, 128), F32)
    out = call(
        second_kernel,
        [VMEM] * 6,
        [plane] * 3,
        [tiles, tiles, scratch, scratch, scratch, dma((9,))],
        COSTS["second"],
        [HBM] * 3,
    )(
        late.reshape(PEERS * 16, 128), forth, back, cut, drop, early
    )
    return tuple(o.reshape(1, ROWS, LINE) for o in out)


COSTS = dict(rows=1, send=100000, start=1, startlow=1, high=100000, low=1, between=1, merge=1, lines=100000, second=1)


def solution(mesh):
    field = P("gz", "xy", None)
    return jax.shard_map(
        local,
        mesh=mesh,
        in_specs=(field,) * 4 + (P(), P()),
        out_specs=(field,) * 3,
        check_vma=False,
    )
```

```python
import jax
import jax.numpy as jnp
from jax import lax
from jax.experimental import pallas as pl
from jax.experimental.pallas import tpu as pltpu
from jax.sharding import PartitionSpec as P

RATE = 4.0
KAPPA = 0.5
ROWS = 32
LINE = 2048
PEERS = 64
HALF = ROWS // 2
TILES = LINE // 128
F32 = jnp.float32
LEVELS = 11
SEGMENT = 8
GROUPS = 8
CUT_LEVELS = 8


def index(shape, axis):
    return lax.broadcasted_iota(jnp.int32, shape, axis)


def swap_blocks(tiles, lane):
    left = lane < 64
    even = (lane & 32) == 0
    half = [None] * 4
    for low in range(2):
        a, b = tiles[low], tiles[low + 2]
        half[low] = jnp.where(left, a, pltpu.roll(b, 64, 1))
        half[low + 2] = jnp.where(left, pltpu.roll(a, 64, 1), b)
    out = [None] * 4
    for high in (0, 2):
        a, b = half[high], half[high + 1]
        out[high] = jnp.where(even, a, pltpu.roll(b, 32, 1))
        out[high + 1] = jnp.where(even, pltpu.roll(a, 96, 1), b)
    return out


def pack(source, target, first):
    lane = index((8, 128), 1)
    for q in range(TILES):
        tiles = [source[8 * u : 8 * u + 8, 128 * q : 128 * q + 128] for u in range(4)]
        for b, tile in enumerate(swap_blocks(tiles, lane)):
            target[4 * q + b, first : first + 8, :] = tile


def pack_turned(source, target, first):
    lane = index((8, 128), 1)
    for wide in range(4):
        square = jnp.concatenate(
            [source[:, 512 * wide + 128 * q : 512 * wide + 128 * q + 128] for q in range(4)], axis=0
        ).T
        for b in range(4):
            tiles = [square[32 * b + 8 * t : 32 * b + 8 * t + 8, :] for t in range(4)]
            for q, tile in enumerate(swap_blocks(tiles, lane)):
                target[16 * wide + 4 * q + b, first : first + 8, :] = tile


def unpack_turned(tile_of, target, lane):
    for g in range(TILES):
        for t, tile in enumerate(swap_blocks([tile_of(4 * g + s) for s in range(4)], lane)):
            target[8 * t : 8 * t + 8, 128 * g : 128 * g + 128] = tile


def turned(tile_of, lane):
    for wide in range(4):
        columns = []
        for s in range(4):
            columns += swap_blocks([tile_of(16 * wide + 4 * g + s) for g in range(4)], lane)
        square = jnp.concatenate(columns, axis=0).T
        for g in range(4):
            yield 128 * (4 * wide + g), square[32 * g : 32 * g + 32, :]


def from_before(values, step, lane):
    if step >= 128:
        jump = step // 128
        return [None] * jump + values[: TILES - jump]
    moved = [pltpu.roll(v, step, 1) for v in values]
    edge = lane < step
    return [jnp.where(edge, moved[k - 1] if k else 0.0, moved[k]) for k in range(TILES)]


def from_after(values, step, lane, wrap=False):
    if step >= 128:
        jump = step // 128
        return values[jump:] + [None] * jump
    moved = [pltpu.roll(v, 128 - step, 1) for v in values]
    edge = lane >= 128 - step
    moved.append(moved[0] if wrap else 0.0)
    return [jnp.where(edge, moved[k + 1], moved[k]) for k in range(TILES)]


def cut_before(values, step):
    if step >= 32:
        jump = step // 32
        return [None] * jump + values[: GROUPS - jump]
    row, lane = index((8, 128), 0), index((8, 128), 1)
    if step >= 4:
        count = step // 4
        moved = [pltpu.roll(v, count, 0) for v in values]
        edge = row < count
        return [jnp.where(edge, moved[k - 1] if k else 0.0, moved[k]) for k in range(GROUPS)]
    aside = [pltpu.roll(v, 32 * step, 1) for v in values]
    moved = [pltpu.roll(v, 1, 0) for v in aside]
    edge = row < 1
    return [
        jnp.where(
            lane < 32 * step,
            jnp.where(edge, moved[k - 1] if k else 0.0, moved[k]),
            aside[k],
        )
        for k in range(GROUPS)
    ]


def cut_after(values, step, wrap=False):
    if step >= 32:
        jump = step // 32
        return values[jump:] + [None] * jump
    row, lane = index((8, 128), 0), index((8, 128), 1)
    if step >= 4:
        count = step // 4
        moved = [pltpu.roll(v, 8 - count, 0) for v in values] + [0.0]
        edge = row >= 8 - count
        return [jnp.where(edge, moved[k + 1], moved[k]) for k in range(GROUPS)]
    aside = [pltpu.roll(v, 128 - 32 * step, 1) for v in values]
    moved = [pltpu.roll(v, 7, 0) for v in aside]
    moved.append(moved[0] if wrap else 0.0)
    edge = row >= 7
    return [
        jnp.where(
            lane >= 128 - 32 * step, jnp.where(edge, moved[k + 1], moved[k]), aside[k]
        )
        for k in range(GROUPS)
    ]


def minus(a, b):
    return a if b is None else a - b


def times(a, b):
    return None if a is None or b is None else a * b


def read(ref):
    return [ref[:, 128 * k : 128 * k + 128] for k in range(TILES)]


def write(ref, values):
    for k, v in enumerate(values):
        ref[:, 128 * k : 128 * k + 128] = v


def factor_level(diagonal, couple, step, before, after):
    weight = [1.0 / d for d in diagonal]
    pull = [times(w, c) for w, c in zip(weight, couple)]
    low = [times(c, w) for c, w in zip(couple, before(weight, step))]
    high = after(pull, step)
    loss = after([times(c, g) for c, g in zip(couple, pull)], step)
    diagonal = [
        minus(minus(d, times(c, a)), b) for d, c, a, b in zip(diagonal, couple, low, loss)
    ]
    couple = [times(a, c) for a, c in zip(low, before(couple, step))]
    return diagonal, couple, low, high


def reduce_level(right, low, high, step, before, after):
    out = []
    for r, a, b, x, y in zip(right, low, high, before(right, step), after(right, step)):
        if x is not None:
            r = r + a * x
        if y is not None:
            r = r + b * y
        out.append(r)
    return out


def factor_lines(diagonal, lane, coef_ref):
    def store(at, values):
        for k, v in enumerate(values):
            if v is not None:
                coef_ref[at, :, 128 * k : 128 * k + 128] = v

    def before(values, step):
        return from_before(values, step, lane)

    def after(values, step):
        return from_after(values, step, lane)

    square = RATE * RATE
    weight = [1.0 / d for d in diagonal]
    left, right = before(weight, 1), after(weight, 1)
    store(0, [RATE * w for w in left])
    store(1, [RATE * w for w in right])
    diagonal = [d - square * (a + b) for d, a, b in zip(diagonal, left, right)]
    couple = [square * w for w in left]
    couple[0] = jnp.where(lane >= 2, couple[0], 0.0)
    for level in range(1, LEVELS):
        diagonal, couple, low, high = factor_level(diagonal, couple, 1 << level, before, after)
        store(2 * level, low)
        store(2 * level + 1, high)
    store(2 * LEVELS, [1.0 / d for d in diagonal])


def reduce_lines(right, lane, coef_ref):
    def load(at):
        return [coef_ref[at, :, 128 * k : 128 * k + 128] for k in range(TILES)]

    def before(values, step):
        return from_before(values, step, lane)

    def after(values, step):
        return from_after(values, step, lane)

    for level in range(LEVELS):
        right = reduce_level(right, load(2 * level), load(2 * level + 1), 1 << level, before, after)
    return [r * w for r, w in zip(right, load(2 * LEVELS))]


def rows_kernel(e_hbm, hx_hbm, below_ref, e_ref, hx_ref, sem):
    copies = [
        pltpu.make_async_copy(e_hbm, e_ref, sem.at[0]),
        pltpu.make_async_copy(hx_hbm, hx_ref, sem.at[1]),
    ]
    for c in copies:
        c.start()
    for c in copies:
        c.wait()
    below_ref[0:1, :] = hx_ref[ROWS - 1 : ROWS, :]
    below_ref[1:2, :] = e_ref[ROWS - 1 : ROWS, :]


def send_kernel(
    region_hbm, eps_hbm, sig_hbm, e_ref, hx_ref, below_ref,
    early_hbm, dplus_ref, dminus_ref,
    region_ref, eps_ref, sig_ref, shifted_ref, tiles_ref, sem,
):
    copies = [
        pltpu.make_async_copy(eps_hbm, eps_ref, sem.at[0]),
        pltpu.make_async_copy(sig_hbm, sig_ref, sem.at[1]),
        pltpu.make_async_copy(region_hbm, region_ref, sem.at[2]),
    ]
    for c in copies:
        c.start()
    row = index((ROWS, 128), 0)
    inside = lax.axis_index("xy") > 0
    for k in range(TILES):
        at = pl.ds(128 * k, 128)
        e = e_ref[:, at]
        edge = below_ref[0:1, at] - RATE * (jnp.where(inside, e[0:1], 0.0) - below_ref[1:2, at])
        half_hx = hx_ref[:, at] - RATE * (pltpu.roll(e, ROWS - 1, 0) - e)
        shifted_ref[:, at] = jnp.where(row == 0, edge, pltpu.roll(half_hx, 1, 0))
    pack(shifted_ref, tiles_ref.at[1], 0)
    sends = [
        pltpu.make_async_copy(tiles_ref.at[i], early_hbm.at[:, pl.ds(8 * i, 8), :], sem.at[3 + i])
        for i in range(2)
    ]
    sends[1].start()
    for c in copies:
        c.wait()
    plus_table = []
    minus_table = []
    for entry in range(8):
        eps = eps_ref[entry] / RATE
        sig = 0.5 * sig_ref[entry]
        plus_table.append(eps + sig)
        minus_table.append(eps - sig)
    for k, here in enumerate(read(region_ref)):
        at = pl.ds(128 * k, 128)
        a = jnp.full((ROWS, 128), plus_table[0])
        b = jnp.full((ROWS, 128), minus_table[0])
        for entry in range(1, 8):
            mask = here == entry
            a = jnp.where(mask, plus_table[entry], a)
            b = jnp.where(mask, minus_table[entry], b)
        dplus_ref[:, at] = a
        dminus_ref[:, at] = b
    pack(dplus_ref, tiles_ref.at[0], 0)
    sends[0].start()
    sends[0].wait()
    sends[1].wait()


def base_of(low, lane, dminus_ref, e_ref, hx_ref, hy_ref, below_ref, base_ref):
    rows = slice(0, HALF) if low else slice(HALF, ROWS)
    row = index((HALF, 128), 0)
    inside = lax.axis_index("xy") > 0
    hy = [hy_ref[rows, 128 * k : 128 * k + 128] for k in range(TILES)]
    hy_before = from_before(hy, 1, lane)
    for k in range(TILES):
        at = slice(128 * k, 128 * k + 128)
        hx = hx_ref[rows, at]
        edge = jnp.where(inside, below_ref[0:1, at], 0.0) if low else hx_ref[HALF - 1 : HALF, at]
        hx_before = jnp.where(row == 0, edge, pltpu.roll(hx, 1, 0))
        e = e_ref[rows, at]
        base_ref[:, at] = (
            dminus_ref[rows, at] * e + (hy[k] - hy_before[k]) - (hx - hx_before) - (2.0 * KAPPA) * e
        )


def diagonal_of(rows, lane, dplus_ref):
    return [
        dplus_ref[rows, 128 * k : 128 * k + 128] + (2.0 * RATE if k else jnp.where(lane > 0, 2.0 * RATE, RATE))
        for k in range(TILES)
    ]


def start_high_kernel(
    dplus_ref, dminus_ref, e_ref, hx_ref, hy_hbm, coef_ref, base_ref, hy_ref, sem
):
    copy = pltpu.make_async_copy(hy_hbm, hy_ref, sem)
    copy.start()
    lane = index((HALF, 128), 1)
    factor_lines(diagonal_of(slice(HALF, ROWS), lane, dplus_ref), lane, coef_ref)
    copy.wait()
    base_of(False, lane, dminus_ref, e_ref, hx_ref, hy_ref, None, base_ref)


def start_low_kernel(
    dplus_ref, dminus_ref, e_ref, hx_ref, hy_ref, below_ref, done_ref, coef_ref, base_ref
):
    lane = index((HALF, 128), 1)
    factor_lines(diagonal_of(slice(0, HALF), lane, dplus_ref), lane, coef_ref)
    base_of(True, lane, dminus_ref, e_ref, hx_ref, hy_ref, below_ref, base_ref)


def halo(one, two):
    layer = lax.axis_index("gz")
    inner = (layer > 0) & (layer < lax.axis_size("gz") - 1)
    return two + jnp.where(inner, one, 0.0)


def half_kernel(low, base_ref, one_ref, two_ref, coef_ref, half_ref):
    lane = index((HALF, 128), 1)
    rows = slice(0, HALF) if low else slice(HALF, ROWS)
    right = []
    for k in range(TILES):
        at = slice(128 * k, 128 * k + 128)
        right.append(base_ref[:, at] + KAPPA * halo(one_ref[rows, at], two_ref[rows, at]))
    write(half_ref, reduce_lines(right, lane, coef_ref))


def high_kernel(*refs):
    half_kernel(False, *refs)


def low_kernel(*refs):
    half_kernel(True, *refs)


def between_kernel(
    half_low_ref, half_high_ref, dminus_ref, hy_ref, one_ref, two_ref,
    base_ref, full_hy_ref, h_scr,
):
    lane = index((ROWS, 128), 1)
    half = [jnp.concatenate(pair, axis=0) for pair in zip(read(half_low_ref), read(half_high_ref))]
    change = [RATE * (a - h) for a, h in zip(from_after(half, 1, lane), half)]
    half_hy = [a + b for a, b in zip(read(hy_ref), change)]
    write(h_scr, [a + b for a, b in zip(half_hy, change)])
    pack_turned(h_scr, full_hy_ref, 0)
    hy_before = from_before(half_hy, 1, lane)
    for k, (m, h) in enumerate(zip(read(dminus_ref), half)):
        at = pl.ds(128 * k, 128)
        right = m * h + (half_hy[k] - hy_before[k]) - (2.0 * KAPPA) * h
        base_ref[0:HALF, at] = right[0:HALF]
        base_ref[HALF:ROWS, at] = right[HALF:ROWS] + KAPPA * halo(one_ref[:, at], two_ref[:, at])


def merge_kernel(hy_ref, base_ref, one_ref, two_ref, done_ref, late_ref, r_scr):
    late_ref[:, 8:16, :] = hy_ref[...]
    r_scr[0:HALF, :] = base_ref[0:HALF, :] + KAPPA * halo(one_ref[...], two_ref[...])
    r_scr[HALF:ROWS, :] = base_ref[HALF:ROWS, :]
    pack(r_scr, late_ref, 0)


def lines_kernel(early_ref, forth_ref, back_ref, cut_ref, drop_ref):
    lane = index((8, 128), 1)
    row = index((8, 128), 0)

    def cells(which, v):
        return [early_ref[pl.ds(128 * g + 8 * which + v, 8, stride=16), :] for g in range(GROUPS)]

    def put(ref, at, values):
        for g, value in enumerate(values):
            if value is not None:
                ref[at, 8 * g : 8 * g + 8, :] = value

    first_segment = (row == 0) & (lane < 32)
    shifted = [cells(1, v) for v in range(SEGMENT)]
    after = cut_after(shifted[0], 1, wrap=True)
    shifted.append(after)
    for v in range(SEGMENT):
        before = list(shifted[v])
        if v == 0:
            before[0] = jnp.where(first_segment, 0.0, before[0])
        put(drop_ref, v, [a - b for a, b in zip(shifted[v + 1], before)])

    diagonal = [[d + 2.0 * RATE for d in cells(0, v)] for v in range(SEGMENT)]
    diagonal[0][0] = diagonal[0][0] - jnp.where(first_segment, RATE, 0.0)
    inner = SEGMENT - 1
    forth = [RATE / d for d in diagonal[0]]
    put(forth_ref, 0, forth)
    product = forth
    for v in range(1, inner):
        forth = [RATE / (d - RATE * p) for d, p in zip(diagonal[v], forth)]
        put(forth_ref, v, forth)
        product = [a * b for a, b in zip(product, forth)]
    back = [RATE / d for d in diagonal[inner - 1]]
    put(back_ref, inner - 1, back)
    for v in range(inner - 2, -1, -1):
        back = [RATE / (d - RATE * p) for d, p in zip(diagonal[v], back)]
        put(back_ref, v, back)
    couple = [RATE * p for p in product]
    couple[0] = jnp.where(first_segment, 0.0, couple[0])
    diagonal = [
        d - RATE * (a + b) for d, a, b in zip(diagonal[inner], forth, cut_after(back, 1))
    ]
    for level in range(CUT_LEVELS):
        diagonal, couple, low, high = factor_level(
            diagonal, couple, 1 << level, cut_before, cut_after
        )
        put(cut_ref, 2 * level, low)
        put(cut_ref, 2 * level + 1, high)
    put(cut_ref, 2 * CUT_LEVELS, [1.0 / d for d in diagonal])


def second_kernel(
    late_ref, forth_ref, back_ref, cut_ref, drop_ref, early_ref, e_hbm, hx_hbm, hy_hbm,
    full_scr, hx_scr, e_ref, hx_ref, hy_ref, sem,
):
    lane = index((8, 128), 1)
    unpack_turned(lambda s: late_ref[16 * s + 8 : 16 * s + 16, :], hy_ref, lane)
    copies = [pltpu.make_async_copy(hy_ref, hy_hbm, sem.at[8])]
    copies[0].start()

    def after_hx(v):
        if v == SEGMENT - 1:
            return cut_after([early_ref[pl.ds(128 * g + 8, 8, stride=16), :] for g in range(GROUPS)], 1, wrap=True)
        return [early_ref[pl.ds(128 * g + 8 + v + 1, 8, stride=16), :] for g in range(GROUPS)]

    def get(ref, at):
        return [ref[at, 8 * g : 8 * g + 8, :] for g in range(GROUPS)]

    inner = SEGMENT - 1
    right = [
        [
            late_ref[pl.ds(128 * g + v, 8, stride=16), :] - d
            for g, d in enumerate(get(drop_ref, v))
        ]
        for v in range(SEGMENT)
    ]
    forth = [p * r for p, r in zip(get(forth_ref, 0), right[0])]
    back = [p * r for p, r in zip(get(back_ref, inner - 1), right[inner - 1])]
    for v in range(1, inner):
        forth = [p * (r + u) for p, r, u in zip(get(forth_ref, v), right[v], forth)]
        w = inner - 1 - v
        back = [p * (r + u) for p, r, u in zip(get(back_ref, w), right[w], back)]
    between = [r + a + b for r, a, b in zip(right[inner], forth, cut_after(back, 1))]
    for level in range(CUT_LEVELS):
        between = reduce_level(
            between, get(cut_ref, 2 * level), get(cut_ref, 2 * level + 1), 1 << level, cut_before, cut_after
        )
    between = [r * w for r, w in zip(between, get(cut_ref, 2 * CUT_LEVELS))]

    def store(ref, v, values):
        for g, value in enumerate(values):
            ref[pl.ds(64 * g + v, 8, stride=8), :] = value

    store(full_scr, inner, between)
    scaled = [RATE * s for s in between]
    chain = [cut_before(scaled, 1)]
    for v in range(inner):
        chain.append([p * (r + u) for p, r, u in zip(get(forth_ref, v), right[v], chain[-1])])
    after = scaled
    for v in range(inner - 1, -1, -1):
        here = [u + p * x for u, p, x in zip(chain[v + 1], get(forth_ref, v), after)]
        store(full_scr, v, [x * (1.0 / RATE) for x in here])
        store(hx_scr, v, [h - (a - f) for h, a, f in zip(after_hx(v), after, here)])
        after = here
    after = cut_after(after, 1)
    store(hx_scr, inner, [h - (a - f) for h, a, f in zip(after_hx(inner), after, scaled)])

    for which, (ref, out, source) in enumerate(((e_ref, e_hbm, full_scr), (hx_ref, hx_hbm, hx_scr))):
        for at, block in turned(lambda s: source[8 * s : 8 * s + 8, :], lane):
            ref[:, at : at + 128] = block
            if at % 512 == 384:
                slab = pl.ds(at - 384, 512)
                copies.append(
                    pltpu.make_async_copy(ref.at[:, slab], out.at[:, slab], sem.at[4 * which + at // 512])
                )
                copies[-1].start()
    for copy in copies:
        copy.wait()


VMEM = pl.BlockSpec(memory_space=pltpu.VMEM)
SMEM = pl.BlockSpec(memory_space=pltpu.SMEM)
HBM = pl.BlockSpec(memory_space=pltpu.HBM)


def struct(*shape):
    return jax.ShapeDtypeStruct(shape, F32)


def call(kernel, ins, outs, scratch=(), cost=1, places=None, aliases=None):
    return pl.pallas_call(
        kernel,
        out_shape=tuple(outs),
        in_specs=list(ins),
        out_specs=tuple(places or (VMEM,) * len(outs)),
        input_output_aliases=aliases or {},
        scratch_shapes=list(scratch),
        compiler_params=pltpu.CompilerParams(vmem_limit_bytes=32 * 1024 * 1024),
        cost_estimate=pl.CostEstimate(
            flops=cost * 1000000, bytes_accessed=1000, transcendentals=0
        ),
        name=kernel.__name__,
    )


def exchanged(value):
    return lax.all_to_all(value, "xy", split_axis=0, concat_axis=0, tiled=True)


def beside(value):
    count = lax.axis_size("gz")
    return [
        lax.ppermute(value, "gz", [(i, (i + (1 if (i + first) % 2 == 0 else -1)) % count) for i in range(count)])
        for first in (1, 0)
    ]


def local(electric, magnetic_first, magnetic_second, region, eps, sig):
    plane = struct(ROWS, LINE)
    scratch = pltpu.VMEM((ROWS, LINE), F32)
    dma = pltpu.SemaphoreType.DMA
    e = electric.reshape(ROWS, LINE)
    hx = magnetic_first.reshape(ROWS, LINE)
    hy = magnetic_second.reshape(ROWS, LINE)
    region = region.reshape(ROWS, LINE)

    e, hx, hy, region, eps, sig = (
        pltpu.with_memory_space_constraint(x, pltpu.HBM) for x in (e, hx, hy, region, eps, sig)
    )
    below, e, hx = call(
        rows_kernel, [HBM] * 2, [struct(2, LINE), plane, plane], [dma((2,))], COSTS["rows"]
    )(e, hx)
    one, two = beside(e)
    count = lax.axis_size("xy")
    below = lax.ppermute(below, "xy", [(i, (i + 1) % count) for i in range(count)])
    table = pltpu.SMEM((8,), F32)
    early, dplus, dminus = call(
        send_kernel,
        [HBM] * 3 + [VMEM] * 3,
        [struct(PEERS, 16, 128), plane, plane],
        [pltpu.VMEM((ROWS, LINE), jnp.int32), table, table, scratch, pltpu.VMEM((2, PEERS, 8, 128), F32), dma((5,))],
        COSTS["send"],
        [HBM, VMEM, VMEM],
    )(region, eps, sig, e, hx, below)
    early = exchanged(early)
    half_plane = struct(HALF, LINE)
    coefs = struct(2 * LEVELS + 1, HALF, LINE)
    coef, base, hy = call(
        start_high_kernel, [VMEM] * 4 + [HBM], [coefs, half_plane, plane], [dma], COSTS["start"]
    )(dplus, dminus, e, hx, hy)
    (half_high,) = call(high_kernel, [VMEM] * 4, [half_plane], (), COSTS["high"])(base, one, two, coef)
    high_one, high_two = beside(half_high)
    coef, base = call(start_low_kernel, [VMEM] * 7, [coefs, half_plane], (), COSTS["startlow"])(
        dplus, dminus, e, hx, hy, below, half_high
    )
    (half_low,) = call(low_kernel, [VMEM] * 4, [half_plane], (), COSTS["low"])(base, one, two, coef)
    low_one, low_two = beside(half_low)
    base, full_hy = call(
        between_kernel, [VMEM] * 6, [plane, struct(PEERS, 8, 128)], [scratch], COSTS["between"]
    )(half_low, half_high, dminus, hy, high_one, high_two)
    rows = 8 * GROUPS
    early = early.reshape(PEERS * 16, 128)
    forth, back, cut, drop = call(
        lines_kernel,
        [VMEM],
        [
            struct(SEGMENT - 1, rows, 128),
            struct(SEGMENT - 1, rows, 128),
            struct(2 * CUT_LEVELS + 1, rows, 128),
            struct(SEGMENT, rows, 128),
        ],
        (),
        COSTS["lines"],
    )(early)
    (late,) = call(
        merge_kernel, [VMEM] * 4 + [HBM], [struct(PEERS, 16, 128)], [scratch], COSTS["merge"]
    )(full_hy, base, low_one, low_two, drop)
    late = exchanged(late)
    tiles = pltpu.VMEM((PEERS * 8, 128), F32)
    out = call(
        second_kernel,
        [VMEM] * 6,
        [plane] * 3,
        [tiles, tiles, scratch, scratch, scratch, dma((9,))],
        COSTS["second"],
        [HBM] * 3,
    )(
        late.reshape(PEERS * 16, 128), forth, back, cut, drop, early
    )
    return tuple(o.reshape(1, ROWS, LINE) for o in out)


COSTS = dict(rows=1, send=100000, start=1, startlow=1, high=100000, low=1, between=1, merge=1, lines=100000, second=1)


def solution(mesh):
    field = P("gz", "xy", None)
    return jax.shard_map(
        local,
        mesh=mesh,
        in_specs=(field,) * 4 + (P(), P()),
        out_specs=(field,) * 3,
        check_vma=False,
    )
```

```python
import jax
import jax.numpy as jnp
from jax import lax
from jax.experimental import pallas as pl
from jax.experimental.pallas import tpu as pltpu
from jax.sharding import PartitionSpec as P

RATE = 4.0
KAPPA = 0.5
ROWS = 32
LINE = 2048
PEERS = 64
HALF = ROWS // 2
TILES = LINE // 128
F32 = jnp.float32
LEVELS = 11
SEGMENT = 8
GROUPS = 8
CUT_LEVELS = 8


def index(shape, axis):
    return lax.broadcasted_iota(jnp.int32, shape, axis)


def swap_blocks(tiles, lane):
    left = lane < 64
    even = (lane & 32) == 0
    half = [None] * 4
    for low in range(2):
        a, b = tiles[low], tiles[low + 2]
        half[low] = jnp.where(left, a, pltpu.roll(b, 64, 1))
        half[low + 2] = jnp.where(left, pltpu.roll(a, 64, 1), b)
    out = [None] * 4
    for high in (0, 2):
        a, b = half[high], half[high + 1]
        out[high] = jnp.where(even, a, pltpu.roll(b, 32, 1))
        out[high + 1] = jnp.where(even, pltpu.roll(a, 96, 1), b)
    return out


def pack(source, target, first):
    lane = index((8, 128), 1)
    for q in range(TILES):
        tiles = [source[8 * u : 8 * u + 8, 128 * q : 128 * q + 128] for u in range(4)]
        for b, tile in enumerate(swap_blocks(tiles, lane)):
            target[4 * q + b, first : first + 8, :] = tile


def pack_turned(source, target, first):
    lane = index((8, 128), 1)
    for wide in range(4):
        square = jnp.concatenate(
            [source[:, 512 * wide + 128 * q : 512 * wide + 128 * q + 128] for q in range(4)], axis=0
        ).T
        for b in range(4):
            tiles = [square[32 * b + 8 * t : 32 * b + 8 * t + 8, :] for t in range(4)]
            for q, tile in enumerate(swap_blocks(tiles, lane)):
                target[16 * wide + 4 * q + b, first : first + 8, :] = tile


def unpack_turned(tile_of, target, lane):
    for g in range(TILES):
        for t, tile in enumerate(swap_blocks([tile_of(4 * g + s) for s in range(4)], lane)):
            target[8 * t : 8 * t + 8, 128 * g : 128 * g + 128] = tile


def turned(tile_of, lane):
    for wide in range(4):
        columns = []
        for s in range(4):
            columns += swap_blocks([tile_of(16 * wide + 4 * g + s) for g in range(4)], lane)
        square = jnp.concatenate(columns, axis=0).T
        for g in range(4):
            yield 128 * (4 * wide + g), square[32 * g : 32 * g + 32, :]


def from_before(values, step, lane):
    if step >= 128:
        jump = step // 128
        return [None] * jump + values[: TILES - jump]
    moved = [pltpu.roll(v, step, 1) for v in values]
    edge = lane < step
    return [jnp.where(edge, moved[k - 1] if k else 0.0, moved[k]) for k in range(TILES)]


def from_after(values, step, lane, wrap=False):
    if step >= 128:
        jump = step // 128
        return values[jump:] + [None] * jump
    moved = [pltpu.roll(v, 128 - step, 1) for v in values]
    edge = lane >= 128 - step
    moved.append(moved[0] if wrap else 0.0)
    return [jnp.where(edge, moved[k + 1], moved[k]) for k in range(TILES)]


def cut_before(values, step):
    if step >= 32:
        jump = step // 32
        return [None] * jump + values[: GROUPS - jump]
    row, lane = index((8, 128), 0), index((8, 128), 1)
    if step >= 4:
        count = step // 4
        moved = [pltpu.roll(v, count, 0) for v in values]
        edge = row < count
        return [jnp.where(edge, moved[k - 1] if k else 0.0, moved[k]) for k in range(GROUPS)]
    aside = [pltpu.roll(v, 32 * step, 1) for v in values]
    moved = [pltpu.roll(v, 1, 0) for v in aside]
    edge = row < 1
    return [
        jnp.where(
            lane < 32 * step,
            jnp.where(edge, moved[k - 1] if k else 0.0, moved[k]),
            aside[k],
        )
        for k in range(GROUPS)
    ]


def cut_after(values, step, wrap=False):
    if step >= 32:
        jump = step // 32
        return values[jump:] + [None] * jump
    row, lane = index((8, 128), 0), index((8, 128), 1)
    if step >= 4:
        count = step // 4
        moved = [pltpu.roll(v, 8 - count, 0) for v in values] + [0.0]
        edge = row >= 8 - count
        return [jnp.where(edge, moved[k + 1], moved[k]) for k in range(GROUPS)]
    aside = [pltpu.roll(v, 128 - 32 * step, 1) for v in values]
    moved = [pltpu.roll(v, 7, 0) for v in aside]
    moved.append(moved[0] if wrap else 0.0)
    edge = row >= 7
    return [
        jnp.where(
            lane >= 128 - 32 * step, jnp.where(edge, moved[k + 1], moved[k]), aside[k]
        )
        for k in range(GROUPS)
    ]


def minus(a, b):
    return a if b is None else a - b


def times(a, b):
    return None if a is None or b is None else a * b


def read(ref):
    return [ref[:, 128 * k : 128 * k + 128] for k in range(TILES)]


def write(ref, values):
    for k, v in enumerate(values):
        ref[:, 128 * k : 128 * k + 128] = v


def factor_level(diagonal, couple, step, before, after):
    weight = [1.0 / d for d in diagonal]
    pull = [times(w, c) for w, c in zip(weight, couple)]
    low = [times(c, w) for c, w in zip(couple, before(weight, step))]
    high = after(pull, step)
    loss = after([times(c, g) for c, g in zip(couple, pull)], step)
    diagonal = [
        minus(minus(d, times(c, a)), b) for d, c, a, b in zip(diagonal, couple, low, loss)
    ]
    couple = [times(a, c) for a, c in zip(low, before(couple, step))]
    return diagonal, couple, low, high


def reduce_level(right, low, high, step, before, after):
    out = []
    for r, a, b, x, y in zip(right, low, high, before(right, step), after(right, step)):
        if x is not None:
            r = r + a * x
        if y is not None:
            r = r + b * y
        out.append(r)
    return out


def factor_lines(diagonal, lane, coef_ref):
    def store(at, values):
        for k, v in enumerate(values):
            if v is not None:
                coef_ref[at, :, 128 * k : 128 * k + 128] = v

    def before(values, step):
        return from_before(values, step, lane)

    def after(values, step):
        return from_after(values, step, lane)

    square = RATE * RATE
    weight = [1.0 / d for d in diagonal]
    left, right = before(weight, 1), after(weight, 1)
    store(0, [RATE * w for w in left])
    store(1, [RATE * w for w in right])
    diagonal = [d - square * (a + b) for d, a, b in zip(diagonal, left, right)]
    couple = [square * w for w in left]
    couple[0] = jnp.where(lane >= 2, couple[0], 0.0)
    for level in range(1, LEVELS):
        diagonal, couple, low, high = factor_level(diagonal, couple, 1 << level, before, after)
        store(2 * level, low)
        store(2 * level + 1, high)
    store(2 * LEVELS, [1.0 / d for d in diagonal])


def reduce_lines(right, lane, coef_ref):
    def load(at):
        return [coef_ref[at, :, 128 * k : 128 * k + 128] for k in range(TILES)]

    def before(values, step):
        return from_before(values, step, lane)

    def after(values, step):
        return from_after(values, step, lane)

    for level in range(LEVELS):
        right = reduce_level(right, load(2 * level), load(2 * level + 1), 1 << level, before, after)
    return [r * w for r, w in zip(right, load(2 * LEVELS))]


def solve_lines(diagonal, right, lane):
    def before(values, step):
        return from_before(values, step, lane)

    def after(values, step):
        return from_after(values, step, lane)

    square = RATE * RATE
    weight = [1.0 / d for d in diagonal]
    share = [RATE * w * r for w, r in zip(weight, right)]
    low, high = before(weight, 1), after(weight, 1)
    right = [r + (a + b) for r, a, b in zip(right, before(share, 1), after(share, 1))]
    diagonal = [d - square * (a + b) for d, a, b in zip(diagonal, low, high)]
    couple = [square * w for w in low]
    couple[0] = jnp.where(lane >= 2, couple[0], 0.0)
    for level in range(1, LEVELS):
        diagonal, couple, low, high = factor_level(diagonal, couple, 1 << level, before, after)
        right = reduce_level(right, low, high, 1 << level, before, after)
    return [r / d for r, d in zip(right, diagonal)]


def rows_kernel(e_hbm, hx_hbm, below_ref, e_ref, hx_ref, sem):
    copies = [
        pltpu.make_async_copy(e_hbm, e_ref, sem.at[0]),
        pltpu.make_async_copy(hx_hbm, hx_ref, sem.at[1]),
    ]
    for c in copies:
        c.start()
    for c in copies:
        c.wait()
    below_ref[0:1, :] = hx_ref[ROWS - 1 : ROWS, :]
    below_ref[1:2, :] = e_ref[ROWS - 1 : ROWS, :]


def send_kernel(
    region_hbm, eps_hbm, sig_hbm, e_ref, hx_ref, below_ref,
    early_hbm, dplus_ref, dminus_ref,
    region_ref, eps_ref, sig_ref, shifted_ref, tiles_ref, sem,
):
    copies = [
        pltpu.make_async_copy(eps_hbm, eps_ref, sem.at[0]),
        pltpu.make_async_copy(sig_hbm, sig_ref, sem.at[1]),
        pltpu.make_async_copy(region_hbm, region_ref, sem.at[2]),
    ]
    for c in copies:
        c.start()
    row = index((ROWS, 128), 0)
    inside = lax.axis_index("xy") > 0
    for k in range(TILES):
        at = pl.ds(128 * k, 128)
        e = e_ref[:, at]
        edge = below_ref[0:1, at] - RATE * (jnp.where(inside, e[0:1], 0.0) - below_ref[1:2, at])
        half_hx = hx_ref[:, at] - RATE * (pltpu.roll(e, ROWS - 1, 0) - e)
        shifted_ref[:, at] = jnp.where(row == 0, edge, pltpu.roll(half_hx, 1, 0))
    pack(shifted_ref, tiles_ref.at[1], 0)
    sends = [
        pltpu.make_async_copy(tiles_ref.at[i], early_hbm.at[:, pl.ds(8 * i, 8), :], sem.at[3 + i])
        for i in range(2)
    ]
    sends[1].start()
    for c in copies:
        c.wait()
    plus_table = []
    minus_table = []
    for entry in range(8):
        eps = eps_ref[entry] / RATE
        sig = 0.5 * sig_ref[entry]
        plus_table.append(eps + sig)
        minus_table.append(eps - sig)
    for k, here in enumerate(read(region_ref)):
        at = pl.ds(128 * k, 128)
        a = jnp.full((ROWS, 128), plus_table[0])
        b = jnp.full((ROWS, 128), minus_table[0])
        for entry in range(1, 8):
            mask = here == entry
            a = jnp.where(mask, plus_table[entry], a)
            b = jnp.where(mask, minus_table[entry], b)
        dplus_ref[:, at] = a
        dminus_ref[:, at] = b
    pack(dplus_ref, tiles_ref.at[0], 0)
    sends[0].start()
    sends[0].wait()
    sends[1].wait()


def base_of(low, lane, dminus_ref, e_ref, hx_ref, hy_ref, below_ref, base_ref):
    rows = slice(0, HALF) if low else slice(HALF, ROWS)
    row = index((HALF, 128), 0)
    inside = lax.axis_index("xy") > 0
    hy = [hy_ref[rows, 128 * k : 128 * k + 128] for k in range(TILES)]
    hy_before = from_before(hy, 1, lane)
    for k in range(TILES):
        at = slice(128 * k, 128 * k + 128)
        hx = hx_ref[rows, at]
        edge = jnp.where(inside, below_ref[0:1, at], 0.0) if low else hx_ref[HALF - 1 : HALF, at]
        hx_before = jnp.where(row == 0, edge, pltpu.roll(hx, 1, 0))
        e = e_ref[rows, at]
        base_ref[:, at] = (
            dminus_ref[rows, at] * e + (hy[k] - hy_before[k]) - (hx - hx_before) - (2.0 * KAPPA) * e
        )


def diagonal_of(rows, lane, dplus_ref):
    return [
        dplus_ref[rows, 128 * k : 128 * k + 128] + (2.0 * RATE if k else jnp.where(lane > 0, 2.0 * RATE, RATE))
        for k in range(TILES)
    ]


def start_high_kernel(
    dplus_ref, dminus_ref, e_ref, hx_ref, hy_hbm, coef_ref, base_ref, hy_ref, sem
):
    copy = pltpu.make_async_copy(hy_hbm, hy_ref, sem)
    copy.start()
    lane = index((HALF, 128), 1)
    factor_lines(diagonal_of(slice(HALF, ROWS), lane, dplus_ref), lane, coef_ref)
    copy.wait()
    base_of(False, lane, dminus_ref, e_ref, hx_ref, hy_ref, None, base_ref)


def halo(one, two):
    layer = lax.axis_index("gz")
    inner = (layer > 0) & (layer < lax.axis_size("gz") - 1)
    return two + jnp.where(inner, one, 0.0)


def high_kernel(base_ref, one_ref, two_ref, coef_ref, half_ref):
    lane = index((HALF, 128), 1)
    right = []
    for k in range(TILES):
        at = slice(128 * k, 128 * k + 128)
        right.append(base_ref[:, at] + KAPPA * halo(one_ref[HALF:ROWS, at], two_ref[HALF:ROWS, at]))
    write(half_ref, reduce_lines(right, lane, coef_ref))


def low_kernel(
    dplus_ref, dminus_ref, e_ref, hx_ref, hy_ref, below_ref, one_ref, two_ref, done_ref, half_ref, base_ref
):
    lane = index((HALF, 128), 1)
    base_of(True, lane, dminus_ref, e_ref, hx_ref, hy_ref, below_ref, base_ref)
    right = []
    for k in range(TILES):
        at = slice(128 * k, 128 * k + 128)
        right.append(base_ref[:, at] + KAPPA * halo(one_ref[0:HALF, at], two_ref[0:HALF, at]))
    write(half_ref, solve_lines(diagonal_of(slice(0, HALF), lane, dplus_ref), right, lane))


def between_kernel(
    half_low_ref, half_high_ref, dminus_ref, hy_ref, one_ref, two_ref,
    base_ref, full_hy_ref, h_scr,
):
    lane = index((ROWS, 128), 1)
    half = [jnp.concatenate(pair, axis=0) for pair in zip(read(half_low_ref), read(half_high_ref))]
    change = [RATE * (a - h) for a, h in zip(from_after(half, 1, lane), half)]
    half_hy = [a + b for a, b in zip(read(hy_ref), change)]
    write(h_scr, [a + b for a, b in zip(half_hy, change)])
    pack_turned(h_scr, full_hy_ref, 0)
    hy_before = from_before(half_hy, 1, lane)
    for k, (m, h) in enumerate(zip(read(dminus_ref), half)):
        at = pl.ds(128 * k, 128)
        right = m * h + (half_hy[k] - hy_before[k]) - (2.0 * KAPPA) * h
        base_ref[0:HALF, at] = right[0:HALF]
        base_ref[HALF:ROWS, at] = right[HALF:ROWS] + KAPPA * halo(one_ref[:, at], two_ref[:, at])


def merge_kernel(hy_ref, base_ref, one_ref, two_ref, done_ref, late_ref, r_scr):
    late_ref[:, 8:16, :] = hy_ref[...]
    r_scr[0:HALF, :] = base_ref[0:HALF, :] + KAPPA * halo(one_ref[...], two_ref[...])
    r_scr[HALF:ROWS, :] = base_ref[HALF:ROWS, :]
    pack(r_scr, late_ref, 0)


def lines_kernel(early_ref, forth_ref, back_ref, cut_ref, drop_ref):
    lane = index((8, 128), 1)
    row = index((8, 128), 0)

    def cells(which, v):
        return [early_ref[pl.ds(128 * g + 8 * which + v, 8, stride=16), :] for g in range(GROUPS)]

    def put(ref, at, values):
        for g, value in enumerate(values):
            if value is not None:
                ref[at, 8 * g : 8 * g + 8, :] = value

    first_segment = (row == 0) & (lane < 32)
    shifted = [cells(1, v) for v in range(SEGMENT)]
    after = cut_after(shifted[0], 1, wrap=True)
    shifted.append(after)
    for v in range(SEGMENT):
        before = list(shifted[v])
        if v == 0:
            before[0] = jnp.where(first_segment, 0.0, before[0])
        put(drop_ref, v, [a - b for a, b in zip(shifted[v + 1], before)])

    diagonal = [[d + 2.0 * RATE for d in cells(0, v)] for v in range(SEGMENT)]
    diagonal[0][0] = diagonal[0][0] - jnp.where(first_segment, RATE, 0.0)
    inner = SEGMENT - 1
    forth = [RATE / d for d in diagonal[0]]
    put(forth_ref, 0, forth)
    product = forth
    for v in range(1, inner):
        forth = [RATE / (d - RATE * p) for d, p in zip(diagonal[v], forth)]
        put(forth_ref, v, forth)
        product = [a * b for a, b in zip(product, forth)]
    back = [RATE / d for d in diagonal[inner - 1]]
    put(back_ref, inner - 1, back)
    for v in range(inner - 2, -1, -1):
        back = [RATE / (d - RATE * p) for d, p in zip(diagonal[v], back)]
        put(back_ref, v, back)
    couple = [RATE * p for p in product]
    couple[0] = jnp.where(first_segment, 0.0, couple[0])
    diagonal = [
        d - RATE * (a + b) for d, a, b in zip(diagonal[inner], forth, cut_after(back, 1))
    ]
    for level in range(CUT_LEVELS):
        diagonal, couple, low, high = factor_level(
            diagonal, couple, 1 << level, cut_before, cut_after
        )
        put(cut_ref, 2 * level, low)
        put(cut_ref, 2 * level + 1, high)
    put(cut_ref, 2 * CUT_LEVELS, [1.0 / d for d in diagonal])


def second_kernel(
    late_ref, forth_ref, back_ref, cut_ref, drop_ref, early_ref, e_hbm, hx_hbm, hy_hbm,
    full_scr, hx_scr, e_ref, hx_ref, hy_ref, sem,
):
    lane = index((8, 128), 1)
    unpack_turned(lambda s: late_ref[16 * s + 8 : 16 * s + 16, :], hy_ref, lane)
    copies = [pltpu.make_async_copy(hy_ref, hy_hbm, sem.at[8])]
    copies[0].start()

    def after_hx(v):
        if v == SEGMENT - 1:
            return cut_after([early_ref[pl.ds(128 * g + 8, 8, stride=16), :] for g in range(GROUPS)], 1, wrap=True)
        return [early_ref[pl.ds(128 * g + 8 + v + 1, 8, stride=16), :] for g in range(GROUPS)]

    def get(ref, at):
        return [ref[at, 8 * g : 8 * g + 8, :] for g in range(GROUPS)]

    inner = SEGMENT - 1
    right = [
        [
            late_ref[pl.ds(128 * g + v, 8, stride=16), :] - d
            for g, d in enumerate(get(drop_ref, v))
        ]
        for v in range(SEGMENT)
    ]
    forth = [p * r for p, r in zip(get(forth_ref, 0), right[0])]
    back = [p * r for p, r in zip(get(back_ref, inner - 1), right[inner - 1])]
    for v in range(1, inner):
        forth = [p * (r + u) for p, r, u in zip(get(forth_ref, v), right[v], forth)]
        w = inner - 1 - v
        back = [p * (r + u) for p, r, u in zip(get(back_ref, w), right[w], back)]
    between = [r + a + b for r, a, b in zip(right[inner], forth, cut_after(back, 1))]
    for level in range(CUT_LEVELS):
        between = reduce_level(
            between, get(cut_ref, 2 * level), get(cut_ref, 2 * level + 1), 1 << level, cut_before, cut_after
        )
    between = [r * w for r, w in zip(between, get(cut_ref, 2 * CUT_LEVELS))]

    def store(ref, v, values):
        for g, value in enumerate(values):
            ref[pl.ds(64 * g + v, 8, stride=8), :] = value

    store(full_scr, inner, between)
    scaled = [RATE * s for s in between]
    chain = [cut_before(scaled, 1)]
    for v in range(inner):
        chain.append([p * (r + u) for p, r, u in zip(get(forth_ref, v), right[v], chain[-1])])
    after = scaled
    for v in range(inner - 1, -1, -1):
        here = [u + p * x for u, p, x in zip(chain[v + 1], get(forth_ref, v), after)]
        store(full_scr, v, [x * (1.0 / RATE) for x in here])
        store(hx_scr, v, [h - (a - f) for h, a, f in zip(after_hx(v), after, here)])
        after = here
    after = cut_after(after, 1)
    store(hx_scr, inner, [h - (a - f) for h, a, f in zip(after_hx(inner), after, scaled)])

    for which, (ref, out, source) in enumerate(((e_ref, e_hbm, full_scr), (hx_ref, hx_hbm, hx_scr))):
        for at, block in turned(lambda s: source[8 * s : 8 * s + 8, :], lane):
            ref[:, at : at + 128] = block
            if at % 512 == 384:
                slab = pl.ds(at - 384, 512)
                copies.append(
                    pltpu.make_async_copy(ref.at[:, slab], out.at[:, slab], sem.at[4 * which + at // 512])
                )
                copies[-1].start()
    for copy in copies:
        copy.wait()


VMEM = pl.BlockSpec(memory_space=pltpu.VMEM)
SMEM = pl.BlockSpec(memory_space=pltpu.SMEM)
HBM = pl.BlockSpec(memory_space=pltpu.HBM)


def struct(*shape):
    return jax.ShapeDtypeStruct(shape, F32)


def call(kernel, ins, outs, scratch=(), cost=1, places=None, aliases=None):
    return pl.pallas_call(
        kernel,
        out_shape=tuple(outs),
        in_specs=list(ins),
        out_specs=tuple(places or (VMEM,) * len(outs)),
        input_output_aliases=aliases or {},
        scratch_shapes=list(scratch),
        compiler_params=pltpu.CompilerParams(vmem_limit_bytes=32 * 1024 * 1024),
        cost_estimate=pl.CostEstimate(
            flops=cost * 1000000, bytes_accessed=1000, transcendentals=0
        ),
        name=kernel.__name__,
    )


def exchanged(value):
    return lax.all_to_all(value, "xy", split_axis=0, concat_axis=0, tiled=True)


def beside(value):
    count = lax.axis_size("gz")
    return [
        lax.ppermute(value, "gz", [(i, (i + (1 if (i + first) % 2 == 0 else -1)) % count) for i in range(count)])
        for first in (1, 0)
    ]


def local(electric, magnetic_first, magnetic_second, region, eps, sig):
    plane = struct(ROWS, LINE)
    scratch = pltpu.VMEM((ROWS, LINE), F32)
    dma = pltpu.SemaphoreType.DMA
    e = electric.reshape(ROWS, LINE)
    hx = magnetic_first.reshape(ROWS, LINE)
    hy = magnetic_second.reshape(ROWS, LINE)
    region = region.reshape(ROWS, LINE)

    e, hx, hy, region, eps, sig = (
        pltpu.with_memory_space_constraint(x, pltpu.HBM) for x in (e, hx, hy, region, eps, sig)
    )
    below, e, hx = call(
        rows_kernel, [HBM] * 2, [struct(2, LINE), plane, plane], [dma((2,))], COSTS["rows"]
    )(e, hx)
    one, two = beside(e)
    count = lax.axis_size("xy")
    below = lax.ppermute(below, "xy", [(i, (i + 1) % count) for i in range(count)])
    table = pltpu.SMEM((8,), F32)
    early, dplus, dminus = call(
        send_kernel,
        [HBM] * 3 + [VMEM] * 3,
        [struct(PEERS, 16, 128), plane, plane],
        [pltpu.VMEM((ROWS, LINE), jnp.int32), table, table, scratch, pltpu.VMEM((2, PEERS, 8, 128), F32), dma((5,))],
        COSTS["send"],
        [HBM, VMEM, VMEM],
    )(region, eps, sig, e, hx, below)
    early = exchanged(early)
    half_plane = struct(HALF, LINE)
    coefs = struct(2 * LEVELS + 1, HALF, LINE)
    coef, base, hy = call(
        start_high_kernel, [VMEM] * 4 + [HBM], [coefs, half_plane, plane], [dma], COSTS["start"]
    )(dplus, dminus, e, hx, hy)
    (half_high,) = call(high_kernel, [VMEM] * 4, [half_plane], (), COSTS["high"])(base, one, two, coef)
    high_one, high_two = beside(half_high)
    (half_low,) = call(
        low_kernel, [VMEM] * 9, [half_plane], [pltpu.VMEM((HALF, LINE), F32)], COSTS["low"]
    )(dplus, dminus, e, hx, hy, below, one, two, half_high)
    low_one, low_two = beside(half_low)
    base, full_hy = call(
        between_kernel, [VMEM] * 6, [plane, struct(PEERS, 8, 128)], [scratch], COSTS["between"]
    )(half_low, half_high, dminus, hy, high_one, high_two)
    rows = 8 * GROUPS
    early = early.reshape(PEERS * 16, 128)
    forth, back, cut, drop = call(
        lines_kernel,
        [VMEM],
        [
            struct(SEGMENT - 1, rows, 128),
            struct(SEGMENT - 1, rows, 128),
            struct(2 * CUT_LEVELS + 1, rows, 128),
            struct(SEGMENT, rows, 128),
        ],
        (),
        COSTS["lines"],
    )(early)
    (late,) = call(
        merge_kernel, [VMEM] * 4 + [HBM], [struct(PEERS, 16, 128)], [scratch], COSTS["merge"]
    )(full_hy, base, low_one, low_two, drop)
    late = exchanged(late)
    tiles = pltpu.VMEM((PEERS * 8, 128), F32)
    out = call(
        second_kernel,
        [VMEM] * 6,
        [plane] * 3,
        [tiles, tiles, scratch, scratch, scratch, dma((9,))],
        COSTS["second"],
        [HBM] * 3,
    )(
        late.reshape(PEERS * 16, 128), forth, back, cut, drop, early
    )
    return tuple(o.reshape(1, ROWS, LINE) for o in out)


COSTS = dict(rows=1, send=100000, start=1, high=100000, low=1, between=1, merge=1, lines=100000, second=1)


def solution(mesh):
    field = P("gz", "xy", None)
    return jax.shard_map(
        local,
        mesh=mesh,
        in_specs=(field,) * 4 + (P(), P()),
        out_specs=(field,) * 3,
        check_vma=False,
    )
```

```python
import jax
import jax.numpy as jnp
from jax import lax
from jax.experimental import pallas as pl
from jax.experimental.pallas import tpu as pltpu
from jax.sharding import PartitionSpec as P

RATE = 4.0
KAPPA = 0.5
ROWS = 32
LINE = 2048
PEERS = 64
HALF = ROWS // 2
TILES = LINE // 128
F32 = jnp.float32
LEVELS = 11
SEGMENT = 8
GROUPS = 8
CUT_LEVELS = 8


def index(shape, axis):
    return lax.broadcasted_iota(jnp.int32, shape, axis)


def swap_blocks(tiles, lane):
    left = lane < 64
    even = (lane & 32) == 0
    half = [None] * 4
    for low in range(2):
        a, b = tiles[low], tiles[low + 2]
        half[low] = jnp.where(left, a, pltpu.roll(b, 64, 1))
        half[low + 2] = jnp.where(left, pltpu.roll(a, 64, 1), b)
    out = [None] * 4
    for high in (0, 2):
        a, b = half[high], half[high + 1]
        out[high] = jnp.where(even, a, pltpu.roll(b, 32, 1))
        out[high + 1] = jnp.where(even, pltpu.roll(a, 96, 1), b)
    return out


def pack(source, target, first, tiles=range(TILES)):
    lane = index((8, 128), 1)
    for q in tiles:
        blocks = [source[8 * u : 8 * u + 8, 128 * q : 128 * q + 128] for u in range(4)]
        for b, tile in enumerate(swap_blocks(blocks, lane)):
            target[4 * q + b, first : first + 8, :] = tile


def pack_turned(source, target, first):
    lane = index((8, 128), 1)
    for wide in range(4):
        square = jnp.concatenate(
            [source[:, 512 * wide + 128 * q : 512 * wide + 128 * q + 128] for q in range(4)], axis=0
        ).T
        for b in range(4):
            tiles = [square[32 * b + 8 * t : 32 * b + 8 * t + 8, :] for t in range(4)]
            for q, tile in enumerate(swap_blocks(tiles, lane)):
                target[16 * wide + 4 * q + b, first : first + 8, :] = tile


def unpack_turned(tile_of, target, lane):
    for g in range(TILES):
        for t, tile in enumerate(swap_blocks([tile_of(4 * g + s) for s in range(4)], lane)):
            target[8 * t : 8 * t + 8, 128 * g : 128 * g + 128] = tile


def turned(tile_of, lane):
    for wide in range(4):
        columns = []
        for s in range(4):
            columns += swap_blocks([tile_of(16 * wide + 4 * g + s) for g in range(4)], lane)
        square = jnp.concatenate(columns, axis=0).T
        for g in range(4):
            yield 128 * (4 * wide + g), square[32 * g : 32 * g + 32, :]


def from_before(values, step, lane):
    if step >= 128:
        jump = step // 128
        return [None] * jump + values[: TILES - jump]
    moved = [pltpu.roll(v, step, 1) for v in values]
    edge = lane < step
    return [jnp.where(edge, moved[k - 1] if k else 0.0, moved[k]) for k in range(TILES)]


def from_after(values, step, lane, wrap=False):
    if step >= 128:
        jump = step // 128
        return values[jump:] + [None] * jump
    moved = [pltpu.roll(v, 128 - step, 1) for v in values]
    edge = lane >= 128 - step
    moved.append(moved[0] if wrap else 0.0)
    return [jnp.where(edge, moved[k + 1], moved[k]) for k in range(TILES)]


def cut_before(values, step):
    if step >= 32:
        jump = step // 32
        return [None] * jump + values[: GROUPS - jump]
    row, lane = index((8, 128), 0), index((8, 128), 1)
    if step >= 4:
        count = step // 4
        moved = [pltpu.roll(v, count, 0) for v in values]
        edge = row < count
        return [jnp.where(edge, moved[k - 1] if k else 0.0, moved[k]) for k in range(GROUPS)]
    aside = [pltpu.roll(v, 32 * step, 1) for v in values]
    moved = [pltpu.roll(v, 1, 0) for v in aside]
    edge = row < 1
    return [
        jnp.where(
            lane < 32 * step,
            jnp.where(edge, moved[k - 1] if k else 0.0, moved[k]),
            aside[k],
        )
        for k in range(GROUPS)
    ]


def cut_after(values, step, wrap=False):
    if step >= 32:
        jump = step // 32
        return values[jump:] + [None] * jump
    row, lane = index((8, 128), 0), index((8, 128), 1)
    if step >= 4:
        count = step // 4
        moved = [pltpu.roll(v, 8 - count, 0) for v in values] + [0.0]
        edge = row >= 8 - count
        return [jnp.where(edge, moved[k + 1], moved[k]) for k in range(GROUPS)]
    aside = [pltpu.roll(v, 128 - 32 * step, 1) for v in values]
    moved = [pltpu.roll(v, 7, 0) for v in aside]
    moved.append(moved[0] if wrap else 0.0)
    edge = row >= 7
    return [
        jnp.where(
            lane >= 128 - 32 * step, jnp.where(edge, moved[k + 1], moved[k]), aside[k]
        )
        for k in range(GROUPS)
    ]


def minus(a, b):
    return a if b is None else a - b


def times(a, b):
    return None if a is None or b is None else a * b


def read(ref):
    return [ref[:, 128 * k : 128 * k + 128] for k in range(TILES)]


def write(ref, values):
    for k, v in enumerate(values):
        ref[:, 128 * k : 128 * k + 128] = v


def factor_level(diagonal, couple, step, before, after):
    weight = [1.0 / d for d in diagonal]
    pull = [times(w, c) for w, c in zip(weight, couple)]
    low = [times(c, w) for c, w in zip(couple, before(weight, step))]
    high = after(pull, step)
    loss = after([times(c, g) for c, g in zip(couple, pull)], step)
    diagonal = [
        minus(minus(d, times(c, a)), b) for d, c, a, b in zip(diagonal, couple, low, loss)
    ]
    couple = [times(a, c) for a, c in zip(low, before(couple, step))]
    return diagonal, couple, low, high


def reduce_level(right, low, high, step, before, after):
    out = []
    for r, a, b, x, y in zip(right, low, high, before(right, step), after(right, step)):
        if x is not None:
            r = r + a * x
        if y is not None:
            r = r + b * y
        out.append(r)
    return out


def factor_lines(diagonal, lane, coef_ref):
    def store(at, values):
        for k, v in enumerate(values):
            if v is not None:
                coef_ref[at, :, 128 * k : 128 * k + 128] = v

    def before(values, step):
        return from_before(values, step, lane)

    def after(values, step):
        return from_after(values, step, lane)

    square = RATE * RATE
    weight = [1.0 / d for d in diagonal]
    left, right = before(weight, 1), after(weight, 1)
    store(0, [RATE * w for w in left])
    store(1, [RATE * w for w in right])
    diagonal = [d - square * (a + b) for d, a, b in zip(diagonal, left, right)]
    couple = [square * w for w in left]
    couple[0] = jnp.where(lane >= 2, couple[0], 0.0)
    for level in range(1, LEVELS):
        diagonal, couple, low, high = factor_level(diagonal, couple, 1 << level, before, after)
        store(2 * level, low)
        store(2 * level + 1, high)
    store(2 * LEVELS, [1.0 / d for d in diagonal])


def reduce_lines(right, lane, coef_ref):
    def load(at):
        return [coef_ref[at, :, 128 * k : 128 * k + 128] for k in range(TILES)]

    def before(values, step):
        return from_before(values, step, lane)

    def after(values, step):
        return from_after(values, step, lane)

    for level in range(LEVELS):
        right = reduce_level(right, load(2 * level), load(2 * level + 1), 1 << level, before, after)
    return [r * w for r, w in zip(right, load(2 * LEVELS))]


def solve_lines(diagonal, right, lane):
    def before(values, step):
        return from_before(values, step, lane)

    def after(values, step):
        return from_after(values, step, lane)

    square = RATE * RATE
    weight = [1.0 / d for d in diagonal]
    share = [RATE * w * r for w, r in zip(weight, right)]
    low, high = before(weight, 1), after(weight, 1)
    right = [r + (a + b) for r, a, b in zip(right, before(share, 1), after(share, 1))]
    diagonal = [d - square * (a + b) for d, a, b in zip(diagonal, low, high)]
    couple = [square * w for w in low]
    couple[0] = jnp.where(lane >= 2, couple[0], 0.0)
    for level in range(1, LEVELS):
        diagonal, couple, low, high = factor_level(diagonal, couple, 1 << level, before, after)
        right = reduce_level(right, low, high, 1 << level, before, after)
    return [r / d for r, d in zip(right, diagonal)]


def rows_kernel(e_hbm, hx_hbm, below_ref, e_ref, hx_ref, sem):
    copies = [
        pltpu.make_async_copy(e_hbm, e_ref, sem.at[0]),
        pltpu.make_async_copy(hx_hbm, hx_ref, sem.at[1]),
    ]
    for c in copies:
        c.start()
    for c in copies:
        c.wait()
    below_ref[0:1, :] = hx_ref[ROWS - 1 : ROWS, :]
    below_ref[1:2, :] = e_ref[ROWS - 1 : ROWS, :]


def send_kernel(
    region_hbm, eps_hbm, sig_hbm, e_ref, hx_ref, below_ref,
    early_hbm, dplus_ref, dminus_ref,
    region_ref, eps_ref, sig_ref, shifted_ref, tiles_ref, sem,
):
    copies = [
        pltpu.make_async_copy(eps_hbm, eps_ref, sem.at[0]),
        pltpu.make_async_copy(sig_hbm, sig_ref, sem.at[1]),
        pltpu.make_async_copy(region_hbm, region_ref, sem.at[2]),
    ]
    for c in copies:
        c.start()
    row = index((ROWS, 128), 0)
    inside = lax.axis_index("xy") > 0
    for k in range(TILES):
        at = pl.ds(128 * k, 128)
        e = e_ref[:, at]
        edge = below_ref[0:1, at] - RATE * (jnp.where(inside, e[0:1], 0.0) - below_ref[1:2, at])
        half_hx = hx_ref[:, at] - RATE * (pltpu.roll(e, ROWS - 1, 0) - e)
        shifted_ref[:, at] = jnp.where(row == 0, edge, pltpu.roll(half_hx, 1, 0))
    pack(shifted_ref, tiles_ref.at[1], 0)
    sends = [pltpu.make_async_copy(tiles_ref.at[1], early_hbm.at[:, pl.ds(8, 8), :], sem.at[3])]
    sends[0].start()
    for c in copies:
        c.wait()
    plus_table = []
    minus_table = []
    for entry in range(8):
        eps = eps_ref[entry] / RATE
        sig = 0.5 * sig_ref[entry]
        plus_table.append(eps + sig)
        minus_table.append(eps - sig)
    for part in range(2):
        for k in range(8 * part, 8 * part + 8):
            at = pl.ds(128 * k, 128)
            here = region_ref[:, at]
            a = jnp.full((ROWS, 128), plus_table[0])
            b = jnp.full((ROWS, 128), minus_table[0])
            for entry in range(1, 8):
                mask = here == entry
                a = jnp.where(mask, plus_table[entry], a)
                b = jnp.where(mask, minus_table[entry], b)
            dplus_ref[:, at] = a
            dminus_ref[:, at] = b
        pack(dplus_ref, tiles_ref.at[0], 0, range(8 * part, 8 * part + 8))
        where = pl.ds(PEERS // 2 * part, PEERS // 2)
        sends.append(
            pltpu.make_async_copy(tiles_ref.at[0, where], early_hbm.at[where, pl.ds(0, 8), :], sem.at[4 + part])
        )
        sends[-1].start()
    for c in sends:
        c.wait()


def base_of(low, lane, dminus_ref, e_ref, hx_ref, hy_ref, below_ref, base_ref):
    rows = slice(0, HALF) if low else slice(HALF, ROWS)
    row = index((HALF, 128), 0)
    inside = lax.axis_index("xy") > 0
    hy = [hy_ref[rows, 128 * k : 128 * k + 128] for k in range(TILES)]
    hy_before = from_before(hy, 1, lane)
    for k in range(TILES):
        at = slice(128 * k, 128 * k + 128)
        hx = hx_ref[rows, at]
        edge = jnp.where(inside, below_ref[0:1, at], 0.0) if low else hx_ref[HALF - 1 : HALF, at]
        hx_before = jnp.where(row == 0, edge, pltpu.roll(hx, 1, 0))
        e = e_ref[rows, at]
        base_ref[:, at] = (
            dminus_ref[rows, at] * e + (hy[k] - hy_before[k]) - (hx - hx_before) - (2.0 * KAPPA) * e
        )


def diagonal_of(rows, lane, dplus_ref):
    return [
        dplus_ref[rows, 128 * k : 128 * k + 128] + (2.0 * RATE if k else jnp.where(lane > 0, 2.0 * RATE, RATE))
        for k in range(TILES)
    ]


def start_high_kernel(
    dplus_ref, dminus_ref, e_ref, hx_ref, hy_hbm, coef_ref, base_ref, hy_ref, sem
):
    copy = pltpu.make_async_copy(hy_hbm, hy_ref, sem)
    copy.start()
    lane = index((HALF, 128), 1)
    factor_lines(diagonal_of(slice(HALF, ROWS), lane, dplus_ref), lane, coef_ref)
    copy.wait()
    base_of(False, lane, dminus_ref, e_ref, hx_ref, hy_ref, None, base_ref)


def halo(one, two):
    layer = lax.axis_index("gz")
    inner = (layer > 0) & (layer < lax.axis_size("gz") - 1)
    return two + jnp.where(inner, one, 0.0)


def high_kernel(base_ref, one_ref, two_ref, coef_ref, half_ref):
    lane = index((HALF, 128), 1)
    right = []
    for k in range(TILES):
        at = slice(128 * k, 128 * k + 128)
        right.append(base_ref[:, at] + KAPPA * halo(one_ref[HALF:ROWS, at], two_ref[HALF:ROWS, at]))
    write(half_ref, reduce_lines(right, lane, coef_ref))


def low_kernel(
    dplus_ref, dminus_ref, e_ref, hx_ref, hy_ref, below_ref, one_ref, two_ref, done_ref, half_ref, base_ref
):
    lane = index((HALF, 128), 1)
    base_of(True, lane, dminus_ref, e_ref, hx_ref, hy_ref, below_ref, base_ref)
    right = []
    for k in range(TILES):
        at = slice(128 * k, 128 * k + 128)
        right.append(base_ref[:, at] + KAPPA * halo(one_ref[0:HALF, at], two_ref[0:HALF, at]))
    write(half_ref, solve_lines(diagonal_of(slice(0, HALF), lane, dplus_ref), right, lane))


def between_kernel(
    half_low_ref, half_high_ref, dminus_ref, hy_ref, one_ref, two_ref,
    base_ref, full_hy_ref, h_scr,
):
    lane = index((ROWS, 128), 1)
    half = [jnp.concatenate(pair, axis=0) for pair in zip(read(half_low_ref), read(half_high_ref))]
    change = [RATE * (a - h) for a, h in zip(from_after(half, 1, lane), half)]
    half_hy = [a + b for a, b in zip(read(hy_ref), change)]
    write(h_scr, [a + b for a, b in zip(half_hy, change)])
    pack_turned(h_scr, full_hy_ref, 0)
    hy_before = from_before(half_hy, 1, lane)
    for k, (m, h) in enumerate(zip(read(dminus_ref), half)):
        at = pl.ds(128 * k, 128)
        right = m * h + (half_hy[k] - hy_before[k]) - (2.0 * KAPPA) * h
        base_ref[0:HALF, at] = right[0:HALF]
        base_ref[HALF:ROWS, at] = right[HALF:ROWS] + KAPPA * halo(one_ref[:, at], two_ref[:, at])


def merge_kernel(hy_ref, base_ref, one_ref, two_ref, done_ref, late_ref, r_scr):
    late_ref[:, 8:16, :] = hy_ref[...]
    r_scr[0:HALF, :] = base_ref[0:HALF, :] + KAPPA * halo(one_ref[...], two_ref[...])
    r_scr[HALF:ROWS, :] = base_ref[HALF:ROWS, :]
    pack(r_scr, late_ref, 0)


def lines_kernel(early_ref, forth_ref, back_ref, cut_ref, drop_ref):
    lane = index((8, 128), 1)
    row = index((8, 128), 0)

    def cells(which, v):
        return [early_ref[pl.ds(128 * g + 8 * which + v, 8, stride=16), :] for g in range(GROUPS)]

    def put(ref, at, values):
        for g, value in enumerate(values):
            if value is not None:
                ref[at, 8 * g : 8 * g + 8, :] = value

    first_segment = (row == 0) & (lane < 32)
    shifted = [cells(1, v) for v in range(SEGMENT)]
    after = cut_after(shifted[0], 1, wrap=True)
    shifted.append(after)
    for v in range(SEGMENT):
        before = list(shifted[v])
        if v == 0:
            before[0] = jnp.where(first_segment, 0.0, before[0])
        put(drop_ref, v, [a - b for a, b in zip(shifted[v + 1], before)])

    diagonal = [[d + 2.0 * RATE for d in cells(0, v)] for v in range(SEGMENT)]
    diagonal[0][0] = diagonal[0][0] - jnp.where(first_segment, RATE, 0.0)
    inner = SEGMENT - 1
    forth = [RATE / d for d in diagonal[0]]
    put(forth_ref, 0, forth)
    product = forth
    for v in range(1, inner):
        forth = [RATE / (d - RATE * p) for d, p in zip(diagonal[v], forth)]
        put(forth_ref, v, forth)
        product = [a * b for a, b in zip(product, forth)]
    back = [RATE / d for d in diagonal[inner - 1]]
    put(back_ref, inner - 1, back)
    for v in range(inner - 2, -1, -1):
        back = [RATE / (d - RATE * p) for d, p in zip(diagonal[v], back)]
        put(back_ref, v, back)
    couple = [RATE * p for p in product]
    couple[0] = jnp.where(first_segment, 0.0, couple[0])
    diagonal = [
        d - RATE * (a + b) for d, a, b in zip(diagonal[inner], forth, cut_after(back, 1))
    ]
    for level in range(CUT_LEVELS):
        diagonal, couple, low, high = factor_level(
            diagonal, couple, 1 << level, cut_before, cut_after
        )
        put(cut_ref, 2 * level, low)
        put(cut_ref, 2 * level + 1, high)
    put(cut_ref, 2 * CUT_LEVELS, [1.0 / d for d in diagonal])


def second_kernel(
    late_ref, forth_ref, back_ref, cut_ref, drop_ref, early_ref, e_hbm, hx_hbm, hy_hbm,
    full_scr, hx_scr, e_ref, hx_ref, hy_ref, sem,
):
    lane = index((8, 128), 1)
    unpack_turned(lambda s: late_ref[16 * s + 8 : 16 * s + 16, :], hy_ref, lane)
    copies = [pltpu.make_async_copy(hy_ref, hy_hbm, sem.at[8])]
    copies[0].start()

    def after_hx(v):
        if v == SEGMENT - 1:
            return cut_after([early_ref[pl.ds(128 * g + 8, 8, stride=16), :] for g in range(GROUPS)], 1, wrap=True)
        return [early_ref[pl.ds(128 * g + 8 + v + 1, 8, stride=16), :] for g in range(GROUPS)]

    def get(ref, at):
        return [ref[at, 8 * g : 8 * g + 8, :] for g in range(GROUPS)]

    inner = SEGMENT - 1
    right = [
        [
            late_ref[pl.ds(128 * g + v, 8, stride=16), :] - d
            for g, d in enumerate(get(drop_ref, v))
        ]
        for v in range(SEGMENT)
    ]
    forth = [p * r for p, r in zip(get(forth_ref, 0), right[0])]
    back = [p * r for p, r in zip(get(back_ref, inner - 1), right[inner - 1])]
    for v in range(1, inner):
        forth = [p * (r + u) for p, r, u in zip(get(forth_ref, v), right[v], forth)]
        w = inner - 1 - v
        back = [p * (r + u) for p, r, u in zip(get(back_ref, w), right[w], back)]
    between = [r + a + b for r, a, b in zip(right[inner], forth, cut_after(back, 1))]
    for level in range(CUT_LEVELS):
        between = reduce_level(
            between, get(cut_ref, 2 * level), get(cut_ref, 2 * level + 1), 1 << level, cut_before, cut_after
        )
    between = [r * w for r, w in zip(between, get(cut_ref, 2 * CUT_LEVELS))]

    def store(ref, v, values):
        for g, value in enumerate(values):
            ref[pl.ds(64 * g + v, 8, stride=8), :] = value

    store(full_scr, inner, between)
    scaled = [RATE * s for s in between]
    chain = [cut_before(scaled, 1)]
    for v in range(inner):
        chain.append([p * (r + u) for p, r, u in zip(get(forth_ref, v), right[v], chain[-1])])
    after = scaled
    for v in range(inner - 1, -1, -1):
        here = [u + p * x for u, p, x in zip(chain[v + 1], get(forth_ref, v), after)]
        store(full_scr, v, [x * (1.0 / RATE) for x in here])
        store(hx_scr, v, [h - (a - f) for h, a, f in zip(after_hx(v), after, here)])
        after = here
    after = cut_after(after, 1)
    store(hx_scr, inner, [h - (a - f) for h, a, f in zip(after_hx(inner), after, scaled)])

    for which, (ref, out, source) in enumerate(((e_ref, e_hbm, full_scr), (hx_ref, hx_hbm, hx_scr))):
        for at, block in turned(lambda s: source[8 * s : 8 * s + 8, :], lane):
            ref[:, at : at + 128] = block
            if at % 512 == 384:
                slab = pl.ds(at - 384, 512)
                copies.append(
                    pltpu.make_async_copy(ref.at[:, slab], out.at[:, slab], sem.at[4 * which + at // 512])
                )
                copies[-1].start()
    for copy in copies:
        copy.wait()


VMEM = pl.BlockSpec(memory_space=pltpu.VMEM)
SMEM = pl.BlockSpec(memory_space=pltpu.SMEM)
HBM = pl.BlockSpec(memory_space=pltpu.HBM)


def struct(*shape):
    return jax.ShapeDtypeStruct(shape, F32)


def call(kernel, ins, outs, scratch=(), cost=1, places=None, aliases=None):
    return pl.pallas_call(
        kernel,
        out_shape=tuple(outs),
        in_specs=list(ins),
        out_specs=tuple(places or (VMEM,) * len(outs)),
        input_output_aliases=aliases or {},
        scratch_shapes=list(scratch),
        compiler_params=pltpu.CompilerParams(vmem_limit_bytes=32 * 1024 * 1024),
        cost_estimate=pl.CostEstimate(
            flops=cost * 1000000, bytes_accessed=1000, transcendentals=0
        ),
        name=kernel.__name__,
    )


def exchanged(value):
    return lax.all_to_all(value, "xy", split_axis=0, concat_axis=0, tiled=True)


def beside(value):
    count = lax.axis_size("gz")
    return [
        lax.ppermute(value, "gz", [(i, (i + (1 if (i + first) % 2 == 0 else -1)) % count) for i in range(count)])
        for first in (1, 0)
    ]


def local(electric, magnetic_first, magnetic_second, region, eps, sig):
    plane = struct(ROWS, LINE)
    scratch = pltpu.VMEM((ROWS, LINE), F32)
    dma = pltpu.SemaphoreType.DMA
    e = electric.reshape(ROWS, LINE)
    hx = magnetic_first.reshape(ROWS, LINE)
    hy = magnetic_second.reshape(ROWS, LINE)
    region = region.reshape(ROWS, LINE)

    e, hx, hy, region, eps, sig = (
        pltpu.with_memory_space_constraint(x, pltpu.HBM) for x in (e, hx, hy, region, eps, sig)
    )
    below, e, hx = call(
        rows_kernel, [HBM] * 2, [struct(2, LINE), plane, plane], [dma((2,))], COSTS["rows"]
    )(e, hx)
    one, two = beside(e)
    count = lax.axis_size("xy")
    below = lax.ppermute(below, "xy", [(i, (i + 1) % count) for i in range(count)])
    table = pltpu.SMEM((8,), F32)
    early, dplus, dminus = call(
        send_kernel,
        [HBM] * 3 + [VMEM] * 3,
        [struct(PEERS, 16, 128), plane, plane],
        [pltpu.VMEM((ROWS, LINE), jnp.int32), table, table, scratch, pltpu.VMEM((2, PEERS, 8, 128), F32), dma((6,))],
        COSTS["send"],
        [HBM, VMEM, VMEM],
    )(region, eps, sig, e, hx, below)
    early = exchanged(early)
    half_plane = struct(HALF, LINE)
    coefs = struct(2 * LEVELS + 1, HALF, LINE)
    coef, base, hy = call(
        start_high_kernel, [VMEM] * 4 + [HBM], [coefs, half_plane, plane], [dma], COSTS["start"]
    )(dplus, dminus, e, hx, hy)
    (half_high,) = call(high_kernel, [VMEM] * 4, [half_plane], (), COSTS["high"])(base, one, two, coef)
    high_one, high_two = beside(half_high)
    (half_low,) = call(
        low_kernel, [VMEM] * 9, [half_plane], [pltpu.VMEM((HALF, LINE), F32)], COSTS["low"]
    )(dplus, dminus, e, hx, hy, below, one, two, half_high)
    low_one, low_two = beside(half_low)
    base, full_hy = call(
        between_kernel, [VMEM] * 6, [plane, struct(PEERS, 8, 128)], [scratch], COSTS["between"]
    )(half_low, half_high, dminus, hy, high_one, high_two)
    rows = 8 * GROUPS
    early = early.reshape(PEERS * 16, 128)
    forth, back, cut, drop = call(
        lines_kernel,
        [VMEM],
        [
            struct(SEGMENT - 1, rows, 128),
            struct(SEGMENT - 1, rows, 128),
            struct(2 * CUT_LEVELS + 1, rows, 128),
            struct(SEGMENT, rows, 128),
        ],
        (),
        COSTS["lines"],
    )(early)
    (late,) = call(
        merge_kernel, [VMEM] * 4 + [HBM], [struct(PEERS, 16, 128)], [scratch], COSTS["merge"]
    )(full_hy, base, low_one, low_two, drop)
    late = exchanged(late)
    tiles = pltpu.VMEM((PEERS * 8, 128), F32)
    out = call(
        second_kernel,
        [VMEM] * 6,
        [plane] * 3,
        [tiles, tiles, scratch, scratch, scratch, dma((9,))],
        COSTS["second"],
        [HBM] * 3,
    )(
        late.reshape(PEERS * 16, 128), forth, back, cut, drop, early
    )
    return tuple(o.reshape(1, ROWS, LINE) for o in out)


COSTS = dict(rows=1, send=100000, start=1, high=100000, low=1, between=1, merge=1, lines=100000, second=1)


def solution(mesh):
    field = P("gz", "xy", None)
    return jax.shard_map(
        local,
        mesh=mesh,
        in_specs=(field,) * 4 + (P(), P()),
        out_specs=(field,) * 3,
        check_vma=False,
    )
```
